32 devices in a mesh: layer: 4 (over y, x), feat: 8 (over z, core).
Axes of the slice: x: 2, y: 2, z: 4, core: 2. Of those that a mesh axis runs over, the one named last changes fastest.
Arguments:
- inputs: bfloat16 [4, 128, 2304], P('layer'), may hold values from -6 to 6
- targets: bfloat16 [4, 128, 2304], P('layer', None, 'feat'), may hold values from -6 to 6
- w_enc: bfloat16 [4, 2304, 2048], P('layer', None, 'feat'), may hold values from -0.125 to 0.125
- b_enc: float32 [4, 2048], P('layer', 'feat'), may hold values from -3 to 3
- w_dec: bfloat16 [4, 4, 2048, 2304], P('layer', None, 'feat'), may hold values from -0.0625 to 0.0625
Outputs:
- grad_enc: bfloat16 [4, 2304, 2048], P('layer', None, 'feat')
- grad_dec: bfloat16 [4, 4, 2048, 2304], P('layer', None, 'feat')
- grad_benc: float32 [4, 2048], P('layer', 'feat')
The draws below stay inside these ranges and needn't reach their ends.
All inputs are finite; a program needn't handle non-finite values.
Results may differ from the reference program's by a relative error of at most 0.0085.
Values may be sent and summed in bfloat16 or wider, within the bound.
No kernel may reach another device: no remote copies, remote signals or barrier semaphores. Data moves between devices by JAX's collectives and lax.ppermute only.
A program may use at most 64 MiB of HBM per device.

```python
import jax
import jax.numpy as jnp
from jax import lax

D = 2304
F = 2048
TOK = 128
LAYERS = 4


def block_levels(stream_key, shape, split, smallest, top_value):
    level = 1.0
    for axis_at, shards_of in split:
        steps = jax.random.uniform(jax.random.fold_in(jax.random.fold_in(stream_key, 6), axis_at), (shards_of,), jnp.float32, smallest / len(split), top_value / len(split))
        level = level * jnp.repeat(jnp.exp(steps), shape[axis_at] // shards_of).reshape((-1,) + (1,) * (len(shape) - 1 - axis_at))
    return level


def bell_draw(key, shape, deviation, reach, shards=(), dtype=jnp.bfloat16):
    array = jax.random.normal(key, shape, jnp.float32) * deviation
    if len(shards) > 0:
        array = block_levels(key, shape, shards, -0.22, 0.18) * array
    return jnp.clip(array, min=-reach, max=reach).astype(dtype)


def setup_inputs(seed: int = 0) -> dict:
    keys = jax.random.split(jax.random.key(seed), 6)
    return {
        "inputs": bell_draw(keys[0], (LAYERS, TOK, D), 1.0, 6.0, ((0, 4),)),
        "targets": bell_draw(keys[1], (LAYERS, TOK, D), 1.0, 6.0, ((0, 4), (2, 8))),
        "w_enc": bell_draw(keys[2], (LAYERS, D, F), D ** -0.5, 0.125, ((0, 4), (2, 8))),
        "b_enc": bell_draw(keys[3], (LAYERS, F), 0.5, 3.0, ((0, 4), (1, 8)), jnp.float32),
        "w_dec": bell_draw(keys[4], (LAYERS, LAYERS, F, D), (F * LAYERS) ** -0.5, 0.0625, ((0, 4), (2, 8))),
    }


def reference(inputs, targets, w_enc, b_enc, w_dec):
    grad_scale = TOK ** -0.5
    layer_count = w_dec.shape[0]
    pre_act = jnp.einsum('ltd,ldf->ltf', inputs.astype(jnp.float32), w_enc.astype(jnp.float32)) + b_enc[:, None, :]
    active = jax.nn.relu(pre_act).astype(jnp.bfloat16)
    layer_ids = jnp.arange(layer_count)

    def recon_of(target_id):
        flag_rows = (layer_ids <= target_id).astype(jnp.float32)
        masked = active.astype(jnp.float32) * flag_rows[:, None, None]
        return jnp.einsum('ltf,lfd->td', masked, w_dec[:, target_id].astype(jnp.float32))

    rebuilt = lax.map(recon_of, layer_ids)
    errors = (rebuilt - targets.astype(jnp.float32)).astype(jnp.bfloat16)

    def source(source_id):
        flag_rows = (layer_ids >= source_id).astype(jnp.float32)
        masked = errors.astype(jnp.float32) * flag_rows[:, None, None]
        weights = w_dec[source_id].astype(jnp.float32)
        act_grad = grad_scale * jnp.einsum('mtd,mfd->tf', masked, weights)
        dec_grad = (grad_scale * jnp.einsum('tf,mtd->mfd', active[source_id].astype(jnp.float32), masked)).astype(jnp.bfloat16)
        return act_grad, dec_grad

    act_grad, grad_dec = lax.map(source, layer_ids)
    pre_grad = jnp.where(pre_act > 0, act_grad, 0.0).astype(jnp.bfloat16)
    grad_enc = jnp.einsum('ltd,ltf->ldf', inputs.astype(jnp.float32), pre_grad.astype(jnp.float32)).astype(jnp.bfloat16)
    grad_benc = jnp.sum(pre_grad.astype(jnp.float32), axis=1)
    return grad_enc, grad_dec, grad_benc
```

```python
import functools

import jax
import jax.numpy as jnp
from jax import lax
from jax.experimental import pallas as pl
from jax.experimental.pallas import tpu as pltpu
from jax.sharding import PartitionSpec as P

F32 = jnp.float32
BF16 = jnp.bfloat16
VMEM_LIMIT = 48 * 1024 * 1024


def slot_offset(slot, core, bits):
    mirrored = 0
    for k in range(bits):
        mirrored = mirrored | (((slot >> k) & 1) << (bits - 1 - k))
    return jnp.where(core == 1, slot, mirrored)


def layer_bit(step, core, bits):
    return bits - 1 - step if core == 1 else step


def call(kernel, grid, in_specs, out_specs, out_shape, flops, nbytes, aliases=None, scratch=()):
    return pl.pallas_call(
        kernel,
        grid_spec=pltpu.PrefetchScalarGridSpec(
            num_scalar_prefetch=1,
            grid=grid,
            in_specs=in_specs,
            out_specs=out_specs,
            scratch_shapes=list(scratch),
        ),
        out_shape=out_shape,
        input_output_aliases=aliases or {},
        compiler_params=pltpu.CompilerParams(
            vmem_limit_bytes=VMEM_LIMIT,
            dimension_semantics=("arbitrary",) * len(grid),
        ),
        cost_estimate=pl.CostEstimate(flops=flops, bytes_accessed=nbytes, transcendentals=0),
    )


def fixed(shape):
    return pl.BlockSpec(shape, lambda *_: (0,) * len(shape))


def encode(pos, x, w_enc, b_enc, w_dec):
    layers, width, cols = w_dec.shape
    toks, half = x.shape[0], cols // 2
    bits = layers.bit_length() - 1

    def target(slot, pos):
        return pos[0] ^ slot_offset(slot, 1 - pos[1], bits)

    def kernel(pos, x_ref, we_ref, b_ref, wd_ref, pre_ref, act_ref, act_t_ref, send_ref):
        slot = pl.program_id(0)

        @pl.when(slot == 0)
        def _():
            pre = jnp.dot(x_ref[...], we_ref[...], preferred_element_type=F32) + b_ref[...]
            pre_ref[...] = pre
            act = jnp.maximum(pre, 0.0).astype(BF16)
            act_ref[...] = act
            act_t_ref[...] = act.T

        live = target(slot, pos) >= pos[0]

        @pl.when(live)
        def _():
            send_ref[0] = jnp.dot(act_ref[...], wd_ref[0], preferred_element_type=F32).astype(BF16)

        @pl.when(jnp.logical_not(live))
        def _():
            send_ref[...] = jnp.zeros_like(send_ref)

    return call(
        kernel,
        (layers,),
        [
            fixed(x.shape),
            fixed(w_enc.shape),
            fixed(b_enc.shape),
            pl.BlockSpec((1, width, half), lambda s, pos: (target(s, pos), 0, 1 - pos[1])),
        ],
        [
            fixed((toks, width)),
            fixed((toks, width)),
            fixed((width, toks)),
            pl.BlockSpec((1, toks, half), lambda s, pos: (s, 0, 0)),
        ],
        [
            jax.ShapeDtypeStruct((toks, width), F32),
            jax.ShapeDtypeStruct((toks, width), BF16),
            jax.ShapeDtypeStruct((width, toks), BF16),
            jax.ShapeDtypeStruct((layers, toks, half), BF16),
        ],
        2 * toks * width * cols + layers * toks * width * cols,
        w_enc.size * 2 + w_dec.size,
    )(pos, x, w_enc, b_enc, w_dec)


def decode_kept(pos, act, w_dec):
    layers, width, cols = w_dec.shape
    toks, half = act.shape[0], cols // 2
    bits = layers.bit_length() - 1

    def target(slot, pos):
        return pos[0] ^ slot_offset(slot, pos[1], bits)

    def kernel(pos, act_ref, wd_ref, keep_ref):
        live = target(pl.program_id(0), pos) >= pos[0]

        @pl.when(live)
        def _():
            keep_ref[0] = jnp.dot(act_ref[...], wd_ref[0], preferred_element_type=F32)

        @pl.when(jnp.logical_not(live))
        def _():
            keep_ref[...] = jnp.zeros_like(keep_ref)

    return call(
        kernel,
        (layers,),
        [
            fixed(act.shape),
            pl.BlockSpec((1, width, half), lambda s, pos: (target(s, pos), 0, pos[1])),
        ],
        pl.BlockSpec((1, toks, half), lambda s, pos: (s, 0, 0)),
        jax.ShapeDtypeStruct((layers, toks, half), F32),
        layers * toks * width * cols,
        w_dec.size,
    )(pos, act, w_dec)


def backward(pos, first, own, other, act_t, w_dec, carry):
    layers, width, cols = w_dec.shape
    count, toks, half = own.shape
    bits = layers.bit_length() - 1
    scale = toks ** (-0.5)

    def side(part, pos):
        return jnp.where(part == 0, pos[1], 1 - pos[1])

    def target(j, part, pos):
        return pos[0] ^ slot_offset(first + j, side(part, pos), bits)

    def kernel(pos, own_ref, oth_ref, act_t_ref, wd_ref, *refs):
        sum_ref, grad_ref = refs[-2:]
        j, part = pl.program_id(0), pl.program_id(1)

        @pl.when((j == 0) & (part == 0))
        def _():
            sum_ref[...] = jnp.zeros_like(sum_ref) if carry is None else refs[0][...]

        live = target(j, part, pos) >= pos[0]

        def work(err):
            sum_ref[...] += lax.dot_general(
                err, wd_ref[0], (((1,), (1,)), ((), ())), preferred_element_type=F32
            )
            grad = jnp.dot(act_t_ref[...], err, preferred_element_type=F32)
            grad_ref[0] = (grad * scale).astype(BF16)

        @pl.when(live & (part == 0))
        def _():
            work(own_ref[0])

        @pl.when(live & (part == 1))
        def _():
            work(oth_ref[0])

        @pl.when(jnp.logical_not(live))
        def _():
            grad_ref[...] = jnp.zeros_like(grad_ref)

    block = pl.BlockSpec(
        (1, width, half), lambda j, part, pos: (target(j, part, pos), 0, side(part, pos))
    )
    err_spec = pl.BlockSpec((1, toks, half), lambda j, part, pos: (j, 0, 0))
    in_specs = [err_spec, err_spec, fixed(act_t.shape), block]
    args = [pos, own, other, act_t, w_dec]
    aliases = {}
    if carry is not None:
        in_specs += [fixed((toks, width)), pl.BlockSpec(memory_space=pl.ANY)]
        args += list(carry)
        aliases = {len(args) - 1: 1}
    return call(
        kernel,
        (count, 2),
        in_specs,
        [fixed((toks, width)), block],
        [jax.ShapeDtypeStruct((toks, width), F32), jax.ShapeDtypeStruct(w_dec.shape, BF16)],
        4 * count * toks * width * cols,
        4 * count * width * cols,
        aliases,
    )(*args)


def encoder_grads(pos, x, pre, act_sum):
    toks, cols = x.shape
    width = pre.shape[1]
    half = cols // 2
    scale = toks ** (-0.5)

    def kernel(pos, x_ref, pre_ref, sum_ref, genc_ref, gb_ref):
        pre_grad = jnp.where(pre_ref[...] > 0, sum_ref[...] * scale, 0.0).astype(BF16)
        genc_ref[...] = lax.dot_general(
            x_ref[...], pre_grad, (((0,), (0,)), ((), ())), preferred_element_type=F32
        ).astype(BF16)
        gb_ref[...] = jnp.sum(pre_grad.astype(F32), axis=0, keepdims=True)

    return call(
        kernel,
        (2,),
        [
            pl.BlockSpec((toks, half), lambda i, pos: (0, i)),
            fixed(pre.shape),
            fixed(act_sum.shape),
        ],
        [pl.BlockSpec((half, width), lambda i, pos: (i, 0)), fixed((1, width))],
        [jax.ShapeDtypeStruct((cols, width), BF16), jax.ShapeDtypeStruct((1, width), F32)],
        2 * toks * cols * width,
        2 * cols * width,
    )(pos, x, pre, act_sum)


def shards(inputs, targets, w_enc, b_enc, w_dec):
    layers, cols = w_dec.shape[1], w_dec.shape[3]
    feats = lax.axis_size("feat")
    bits, feat_bits = layers.bit_length() - 1, feats.bit_length() - 1
    half = cols // 2
    own_layer, own_feat = lax.axis_index("layer"), lax.axis_index("feat")
    core = own_feat & 1
    pos = jnp.stack([own_layer, core]).astype(jnp.int32)
    x, tgt, wd = inputs[0], targets[0], w_dec[0]

    def swap_feat(value, bit):
        return lax.ppermute(value, "feat", [(f, f ^ (1 << bit)) for f in range(feats)])

    def swap_layer(value, step):
        pairs = [
            (l * feats + f, (l ^ (1 << layer_bit(step, f & 1, bits))) * feats + f)
            for l in range(layers)
            for f in range(feats)
        ]
        return lax.ppermute(value, ("layer", "feat"), pairs)

    pre, act, act_t, send = encode(pos, x, w_enc[0], b_enc, wd)
    got = swap_feat(send, 0)
    keep = decode_kept(pos, act, wd)

    pair_tgt = swap_feat(tgt, 0)
    wide = jnp.zeros((x.shape[0], cols), BF16)
    wide = lax.dynamic_update_slice(wide, tgt, (0, own_feat * tgt.shape[1]))
    wide = lax.dynamic_update_slice(wide, pair_tgt, (0, (own_feat ^ 1) * tgt.shape[1]))
    wide = jnp.where(core == 0, wide[:, :half], wide[:, half:])

    slots = [keep[s] + got[s].astype(F32) for s in range(layers)]
    for step in range(bits):
        n = len(slots) // 2
        cut = n // 2
        parts = [(n + cut, 2 * n), (n, n + cut)] if cut else [(n, 2 * n)]
        arrived = {}
        for low, high in parts:
            piece = jnp.stack([slots[s] for s in range(low, high)]).astype(BF16)
            piece = swap_layer(piece, step)
            for s in range(low, high):
                arrived[s - n] = piece[s - low]
        slots = [slots[s] + arrived[s].astype(F32) for s in range(n)]
    rows = slots[0] - wide.astype(F32)

    for bit in range(1, feat_bits - 1):
        n = rows.shape[0] // 2
        high = ((own_feat >> bit) & 1) == 1
        away = jnp.where(high, rows[:n], rows[n:]).astype(BF16)
        rows = jnp.where(high, rows[n:], rows[:n]) + swap_feat(away, bit).astype(F32)
    rows = rows + swap_feat(rows.astype(BF16), feat_bits - 1).astype(F32)
    err = rows.astype(BF16)

    for bit in reversed(range(1, feat_bits - 1)):
        high = ((own_feat >> bit) & 1) == 1
        far = swap_feat(err, bit)
        err = jnp.concatenate([jnp.where(high, far, err), jnp.where(high, err, far)])

    slots = [err]
    own = err[None]
    carry = None
    first = 0
    for step in reversed(range(-1, bits)):
        carry = backward(pos, first, own, swap_feat(own, 0), act_t, wd, carry)
        if step < 0:
            break
        first = len(slots)
        cut = first // 2
        parts = [(0, cut), (cut, first)] if cut else [(0, first)]
        new = []
        for low, high in parts:
            piece = swap_layer(jnp.stack(slots[low:high]), step)
            new += [piece[i] for i in range(high - low)]
        slots = slots + new
        own = jnp.stack(new)
    act_sum, grad_dec = carry
    grad_enc, grad_benc = encoder_grads(pos, x, pre, act_sum)
    return grad_enc[None], grad_dec[None], grad_benc


def solution(mesh):
    in_specs = (
        P("layer", None, None),
        P("layer", None, "feat"),
        P("layer", None, "feat"),
        P("layer", "feat"),
        P("layer", None, "feat", None),
    )
    out_specs = (P("layer", None, "feat"), P("layer", None, "feat", None), P("layer", "feat"))
    return jax.shard_map(shards, mesh=mesh, in_specs=in_specs, out_specs=out_specs, check_vma=False)
```

```python
import jax
import jax.numpy as jnp
from jax import lax
from jax.experimental import pallas as pl
from jax.experimental.pallas import tpu as pltpu
from jax.sharding import PartitionSpec as P

F32 = jnp.float32
BF16 = jnp.bfloat16
VMEM_LIMIT = 16 * 1024 * 1024
IN_VMEM = pl.BlockSpec(memory_space=pltpu.VMEM)
IN_PLACE = pl.BlockSpec(memory_space=pl.ANY)
IN_SMEM = pl.BlockSpec(memory_space=pltpu.SMEM)


def slot_offset(slot, core, bits):
    mirrored = 0
    for k in range(bits):
        mirrored = mirrored | (((slot >> k) & 1) << (bits - 1 - k))
    return jnp.where(core == 1, slot, mirrored)


def layer_bit(step, core, bits):
    return bits - 1 - step if core == 1 else step


def params():
    return dict(
        compiler_params=pltpu.CompilerParams(vmem_limit_bytes=VMEM_LIMIT),
        cost_estimate=pl.CostEstimate(flops=1, bytes_accessed=1, transcendentals=0),
    )


def in_hbm(value):
    return pltpu.with_memory_space_constraint(value, pltpu.HBM)


def in_vmem(value):
    return pltpu.with_memory_space_constraint(value, pltpu.VMEM)


def after(value, *others):
    return lax.optimization_barrier((value, *others))[0]


def weight_copies(pos, jobs, layers, wd_hbm, w_ref, sems):
    half = w_ref.shape[-1]
    bits = layers.bit_length() - 1
    copies, live = [], []
    for i, (slot, part) in enumerate(jobs):
        side = pos[1] if part == 0 else 1 - pos[1]
        target = pos[0] ^ slot_offset(slot, side, bits)
        cols = pl.ds(pl.multiple_of(side * half, half), half)
        copies.append(pltpu.make_async_copy(wd_hbm.at[target, :, cols], w_ref.at[i], sems.at[i]))
        live.append(target >= pos[0])
    return copies, live


def partial_sums(copies, live, act, w_ref, out_refs):
    for i, out_ref in enumerate(out_refs):
        copies[i].wait()

        @pl.when(live[i])
        def _():
            out_ref[...] = jnp.dot(act, w_ref[i], preferred_element_type=F32).astype(out_ref.dtype)

        @pl.when(jnp.logical_not(live[i]))
        def _():
            out_ref[...] = jnp.zeros_like(out_ref)


def job_shapes(jobs, toks, half):
    return [pltpu.VMEM((toks, half), F32 if part == 0 else BF16) for _, part in jobs]


def encode(pos, x, w_enc, b_enc, w_dec, jobs):
    layers, width, cols = w_dec.shape
    toks, half = x.shape[0], cols // 2
    pieces = 3 if cols % (3 * 128) == 0 else 1
    rows = cols // pieces

    def kernel(pos, x_hbm, we_hbm, b_hbm, wd_hbm, pre_ref, act_ref, act_t_ref, *refs):
        out_refs, (w_ref, x_ref, we_ref, b_ref, sems, w_sems) = refs[: len(jobs)], refs[len(jobs):]
        loads = [pltpu.make_async_copy(b_hbm, b_ref, sems.at[0])]
        for i in range(pieces):
            span = pl.ds(i * rows, rows)
            loads.append(pltpu.make_async_copy(x_hbm.at[:, span], x_ref.at[:, span], sems.at[2 * i + 1]))
            loads.append(pltpu.make_async_copy(we_hbm.at[span], we_ref.at[span], sems.at[2 * i + 2]))
        for load in loads:
            load.start()
        copies, live = weight_copies(pos, jobs, layers, wd_hbm, w_ref, w_sems)
        for copy in copies:
            copy.start()
        loads[0].wait()
        pre = jnp.broadcast_to(b_ref[...], (toks, width))
        for i in range(pieces):
            loads[2 * i + 1].wait()
            loads[2 * i + 2].wait()
            span = pl.ds(i * rows, rows)
            pre += jnp.dot(x_ref[:, span], we_ref[span], preferred_element_type=F32)
        pre_ref[...] = pre
        act = jnp.maximum(pre, 0.0).astype(BF16)
        act_ref[...] = act
        partial_sums(copies, live, act, w_ref, out_refs)
        act_t_ref[...] = act.T

    out = pl.pallas_call(
        kernel,
        in_specs=[IN_SMEM] + [IN_PLACE] * 4,
        out_specs=[IN_VMEM] * (3 + len(jobs)),
        out_shape=[
            pltpu.VMEM((toks, width), F32),
            pltpu.VMEM((toks, width), BF16),
            pltpu.VMEM((width, toks), BF16),
        ]
        + job_shapes(jobs, toks, half),
        scratch_shapes=[
            pltpu.VMEM((len(jobs), width, half), BF16),
            pltpu.VMEM(x.shape, BF16),
            pltpu.VMEM(w_enc.shape, BF16),
            pltpu.VMEM(b_enc.shape, F32),
            pltpu.SemaphoreType.DMA((2 * pieces + 1,)),
            pltpu.SemaphoreType.DMA((len(jobs),)),
        ],
        **params(),
    )(pos, in_hbm(x), in_hbm(w_enc), in_hbm(b_enc), in_hbm(w_dec))
    return out[0], out[1], out[2], dict(zip(jobs, out[3:]))


def decode(pos, act, w_dec, jobs):
    layers, width, cols = w_dec.shape
    toks, half = act.shape[0], cols // 2

    def kernel(pos, act_ref, wd_hbm, *refs):
        out_refs, (w_ref, w_sems) = refs[: len(jobs)], refs[len(jobs):]
        copies, live = weight_copies(pos, jobs, layers, wd_hbm, w_ref, w_sems)
        for copy in copies:
            copy.start()
        partial_sums(copies, live, act_ref[...], w_ref, out_refs)

    out = pl.pallas_call(
        kernel,
        in_specs=[IN_SMEM, IN_VMEM, IN_PLACE],
        out_specs=[IN_VMEM] * len(jobs),
        out_shape=job_shapes(jobs, toks, half),
        scratch_shapes=[
            pltpu.VMEM((len(jobs), width, half), BF16),
            pltpu.SemaphoreType.DMA((len(jobs),)),
        ],
        **params(),
    )(pos, in_vmem(act), in_hbm(w_dec))
    return dict(zip(jobs, out))


def backward(pos, slot, errs, act_t, w_dec, carry, last=None):
    layers, width, cols = w_dec.shape
    toks, half = errs[0].shape
    bits = layers.bit_length() - 1
    scale = toks ** (-0.5)
    ahead = slot == layers - 2

    def kernel(pos, *refs):
        err_refs, act_t_ref, wd_hbm, refs = refs[:2], refs[2], refs[3], refs[4:]
        if carry is not None:
            (old_ref, _), refs = refs[:2], refs[2:]
        if last is not None:
            (w_ref, x_ref, pre_ref), refs = refs[:3], refs[3:]
        sum_ref, grad_hbm, refs = refs[0], refs[1], refs[2:]
        if ahead:
            next_ref, refs = refs[0], refs[1:]
        if last is not None:
            (genc_hbm, gb_ref), refs = refs[:2], refs[2:]
        grad_ref, sems, refs = refs[0], refs[1], refs[2:]

        loads, writes, live, prefetch = [], [], [], []
        for part in range(2):
            side = pos[1] if part == 0 else 1 - pos[1]
            target = pos[0] ^ slot_offset(slot, side, bits)
            span = pl.ds(pl.multiple_of(side * half, half), half)
            writes.append(pltpu.make_async_copy(grad_ref.at[part], grad_hbm.at[target, :, span], sems.at[part]))
            live.append(target >= pos[0])
            if last is None:
                loads.append(pltpu.make_async_copy(wd_hbm.at[target, :, span], refs[0].at[part], refs[1].at[part]))
            if ahead:
                target = pos[0] ^ slot_offset(slot + 1, side, bits)
                prefetch.append(pltpu.make_async_copy(wd_hbm.at[target, :, span], next_ref.at[part], refs[1].at[2 + part]))
        if last is None:
            w_ref = refs[0]
        for copy in loads + prefetch:
            copy.start()

        def decoder_part(part):
            @pl.when(live[part])
            def _():
                grad = jnp.dot(act_t_ref[...], err_refs[part][...], preferred_element_type=F32)
                grad_ref[part] = (grad * scale).astype(BF16)

            @pl.when(jnp.logical_not(live[part]))
            def _():
                grad_ref[part] = jnp.zeros((width, half), BF16)

            writes[part].start()

        if last is None:
            decoder_part(0)
            decoder_part(1)
        sum_ref[...] = jnp.zeros_like(sum_ref) if carry is None else old_ref[...]
        for part in range(2):
            if loads:
                loads[part].wait()

            @pl.when(live[part])
            def _():
                sum_ref[...] += lax.dot_general(
                    err_refs[part][...], w_ref[part], (((1,), (1,)), ((), ())), preferred_element_type=F32
                )

        if last is not None:
            genc_ref, enc_sems = refs
            pre_grad = jnp.where(pre_ref[...] > 0, sum_ref[...] * scale, 0.0).astype(BF16)
            gb_ref[...] = jnp.sum(pre_grad.astype(F32), axis=0, keepdims=True)
            for i in range(2):
                span = pl.ds(i * half, half)
                genc_ref[span] = lax.dot_general(
                    x_ref[:, span], pre_grad, (((0,), (0,)), ((), ())), preferred_element_type=F32
                ).astype(BF16)
                write = pltpu.make_async_copy(genc_ref.at[span], genc_hbm.at[span], enc_sems.at[i])
                write.start()
                writes.append(write)
            decoder_part(0)
            decoder_part(1)
        for copy in prefetch + writes:
            copy.wait()

    in_specs = [IN_SMEM] + [IN_VMEM] * 3 + [IN_PLACE]
    args = [pos] + [in_vmem(a) for a in (*errs, act_t)] + [in_hbm(w_dec)]
    out_specs = [IN_VMEM, IN_PLACE]
    out_shape = [pltpu.VMEM((toks, width), F32), pltpu.HBM((layers, width, cols), BF16)]
    scratch = [pltpu.VMEM((2, width, half), BF16), pltpu.SemaphoreType.DMA((2,))]
    aliases = {}
    if carry is not None:
        in_specs += [IN_VMEM, IN_PLACE]
        args += [in_vmem(carry[0]), carry[1]]
        aliases = {len(args) - 1: 1}
    if ahead:
        out_specs += [IN_VMEM]
        out_shape += [pltpu.VMEM((2, width, half), BF16)]
    if last is None:
        scratch += [pltpu.VMEM((2, width, half), BF16), pltpu.SemaphoreType.DMA((4,))]
    else:
        in_specs += [IN_VMEM] * 3
        args += [in_vmem(a) for a in (carry[2], *last)]
        out_specs += [IN_PLACE, IN_VMEM]
        out_shape += [pltpu.HBM((cols, width), BF16), jax.ShapeDtypeStruct((1, width), F32)]
        scratch += [pltpu.VMEM((cols, width), BF16), pltpu.SemaphoreType.DMA((2,))]
    return pl.pallas_call(
        kernel,
        in_specs=in_specs,
        out_specs=out_specs,
        out_shape=out_shape,
        scratch_shapes=scratch,
        input_output_aliases=aliases,
        **params(),
    )(*args)


def add_up(values, dtype):
    def kernel(*refs):
        total = refs[0][...].astype(F32)
        for ref in refs[1:-1]:
            total += ref[...].astype(F32)
        refs[-1][...] = total.astype(dtype)

    return pl.pallas_call(
        kernel,
        in_specs=[IN_VMEM] * len(values),
        out_specs=IN_VMEM,
        out_shape=pltpu.VMEM(values[0].shape, dtype),
        **params(),
    )(*[in_vmem(v) for v in values])


def split_rows(high, minus, values):
    toks, cols = minus.shape
    n = toks // 2

    def kernel(high, minus_ref, *refs):
        def rows(start):
            span = pl.ds(pl.multiple_of(start, n), n)
            total = -minus_ref[span].astype(F32)
            for ref in refs[:-2]:
                total += ref[span].astype(F32)
            return total

        refs[-1][...] = rows((1 - high[0]) * n).astype(BF16)
        refs[-2][...] = rows(high[0] * n)

    return pl.pallas_call(
        kernel,
        in_specs=[IN_SMEM] + [IN_VMEM] * (1 + len(values)),
        out_specs=[IN_VMEM] * 2,
        out_shape=[pltpu.VMEM((n, cols), F32), pltpu.VMEM((n, cols), BF16)],
        **params(),
    )(high, *[in_vmem(v) for v in (minus, *values)])


def shards(inputs, targets, w_enc, b_enc, w_dec):
    layers, cols = w_dec.shape[1], w_dec.shape[3]
    feats = lax.axis_size("feat")
    bits, feat_bits = layers.bit_length() - 1, feats.bit_length() - 1
    half = cols // 2
    own_layer, own_feat = lax.axis_index("layer"), lax.axis_index("feat")
    core = own_feat & 1
    pos = jnp.stack([own_layer, core]).astype(jnp.int32)
    x, tgt, wd = inputs[0], targets[0], w_dec[0]

    def swap_feat(value, bit):
        return lax.ppermute(value, "feat", [(f, f ^ (1 << bit)) for f in range(feats)])

    def swap_layer(value, step):
        pairs = [
            (l * feats + f, (l ^ (1 << layer_bit(step, f & 1, bits))) * feats + f)
            for l in range(layers)
            for f in range(feats)
        ]
        return lax.ppermute(value, ("layer", "feat"), pairs)

    def jobs(low, high):
        return [(s, part) for s in reversed(range(low, high)) for part in (1, 0)]

    mid = layers // 2
    pre, act, act_t, sums = encode(pos, x, w_enc[0], b_enc, wd, jobs(layers - 1, layers))
    got = {layers - 1: swap_feat(sums[layers - 1, 1], 0)}
    sums |= decode(pos, act, wd, jobs(mid, layers - 1))
    for s in reversed(range(mid, layers - 1)):
        got[s] = swap_feat(sums[s, 1], 0)
    away = add_up([after(sums[layers - 1, 0], *[sums[j] for j in jobs(mid, layers - 1)]), got[layers - 1]], BF16)
    arrived = {layers - 1 - mid: swap_layer(away, 0)}
    sums |= decode(pos, after(act, away), wd, jobs(0, mid))
    for s in reversed(range(mid)):
        got[s] = swap_feat(sums[s, 1], 0)
    tgt = after(tgt, away)
    for s in reversed(range(mid, layers - 1)):
        away = add_up([after(sums[s, 0], sums[0, 0]), got[s]], BF16)
        arrived[s - mid] = swap_layer(away, 0)
    slots = [[sums[s, 0], got[s], arrived[s]] for s in range(mid)]
    for step in range(1, bits):
        n = len(slots) // 2
        for s in reversed(range(n)):
            slots[s].append(swap_layer(add_up(slots[n + s], BF16), step))
        slots = slots[:n]

    pair_tgt = swap_feat(tgt, 0)
    pair = jnp.where(core == 0, jnp.stack([tgt, pair_tgt]), jnp.stack([pair_tgt, tgt]))
    pair = jnp.concatenate([pair[0], pair[1]], axis=1)
    span = pair.shape[1]
    chip, chips = own_feat >> 1, feats // 2
    spread = jnp.zeros((x.shape[0], half), BF16)
    for i in range(chips // 2):
        padded = jnp.pad(pair, ((0, 0), (i * span, half - (i + 1) * span)))
        spread = jnp.where(chip == core * (chips // 2) + i, padded, spread)

    for bit in range(1, feat_bits - 1):
        high = (own_feat >> bit) & 1
        if bit == 1:
            rows, away = split_rows(high.reshape(1), spread, slots[0])
        else:
            n = rows.shape[0] // 2
            away = jnp.where(high == 1, rows[:n], rows[n:]).astype(BF16)
            rows = jnp.where(high == 1, rows[n:], rows[:n])
        rows = rows + swap_feat(away, bit).astype(F32)
    rows = rows + swap_feat(rows.astype(BF16), feat_bits - 1).astype(F32)
    err = rows.astype(BF16)

    for bit in reversed(range(1, feat_bits - 1)):
        high = ((own_feat >> bit) & 1) == 1
        far = swap_feat(err, bit)
        err = jnp.concatenate([jnp.where(high, far, err), jnp.where(high, err, far)])

    other = swap_feat(err, 0)
    carry = backward(pos, 0, (err, other), act_t, wd, None)
    slots = [err]
    for step in reversed(range(bits)):
        for s in range(len(slots)):
            value = slots[s]
            if step == 0 and s == 0:
                value = after(value, other)
            elif step == 0 and s == 1:
                value = after(value, carry[0])
            slots.append(swap_layer(value, step))
    for s in range(1, layers):
        own = slots[s]
        if s < layers // 2 + 1:
            own = after(own, slots[layers // 2])
        elif s == layers - 1:
            own = after(own, carry[0])
        last = (x, pre) if s == layers - 1 else None
        carry = backward(pos, s, (own, swap_feat(own, 0)), act_t, wd, carry, last)
    act_sum, grad_dec, grad_enc, grad_benc = carry
    return grad_enc[None], grad_dec[None], grad_benc


def solution(mesh):
    in_specs = (
        P("layer", None, None),
        P("layer", None, "feat"),
        P("layer", None, "feat"),
        P("layer", "feat"),
        P("layer", None, "feat", None),
    )
    out_specs = (P("layer", None, "feat"), P("layer", None, "feat", None), P("layer", "feat"))
    return jax.shard_map(shards, mesh=mesh, in_specs=in_specs, out_specs=out_specs, check_vma=False)
```

```python
import jax
import jax.numpy as jnp
from jax import lax
from jax.experimental import pallas as pl
from jax.experimental.pallas import tpu as pltpu
from jax.sharding import PartitionSpec as P

F32 = jnp.float32
BF16 = jnp.bfloat16
VMEM_LIMIT = 16 * 1024 * 1024
IN_VMEM = pl.BlockSpec(memory_space=pltpu.VMEM)
IN_PLACE = pl.BlockSpec(memory_space=pl.ANY)
IN_SMEM = pl.BlockSpec(memory_space=pltpu.SMEM)


def slot_offset(slot, core, bits):
    mirrored = 0
    for k in range(bits):
        mirrored = mirrored | (((slot >> k) & 1) << (bits - 1 - k))
    return jnp.where(core == 1, slot, mirrored)


def layer_bit(step, core, bits):
    return bits - 1 - step if core == 1 else step


def params(cost=1):
    return dict(
        compiler_params=pltpu.CompilerParams(vmem_limit_bytes=VMEM_LIMIT),
        cost_estimate=pl.CostEstimate(flops=cost, bytes_accessed=1, transcendentals=0),
    )


def in_hbm(value):
    return pltpu.with_memory_space_constraint(value, pltpu.HBM)


def in_vmem(value):
    return pltpu.with_memory_space_constraint(value, pltpu.VMEM)


def after(value, *others):
    return lax.optimization_barrier((value, *others))[0]


def weight_copies(pos, jobs, layers, wd_hbm, w_ref, sems):
    half = w_ref.shape[-1]
    bits = layers.bit_length() - 1
    copies, live = [], []
    for i, (slot, part) in enumerate(jobs):
        side = pos[1] if part == 0 else 1 - pos[1]
        target = pos[0] ^ slot_offset(slot, side, bits)
        cols = pl.ds(pl.multiple_of(side * half, half), half)
        copies.append(pltpu.make_async_copy(wd_hbm.at[target, :, cols], w_ref.at[i], sems.at[i]))
        live.append(target >= pos[0])
    return copies, live


def partial_sums(copies, live, act, w_ref, out_refs):
    for i, out_ref in enumerate(out_refs):
        copies[i].wait()

        @pl.when(live[i])
        def _():
            out_ref[...] = jnp.dot(act, w_ref[i], preferred_element_type=F32).astype(out_ref.dtype)

        @pl.when(jnp.logical_not(live[i]))
        def _():
            out_ref[...] = jnp.zeros_like(out_ref)


def job_shapes(jobs, toks, half):
    return [pltpu.VMEM((toks, half), F32 if part == 0 else BF16) for _, part in jobs]


def encode(pos, x, w_enc, b_enc, w_dec, jobs):
    layers, width, cols = w_dec.shape
    toks, half = x.shape[0], cols // 2
    pieces = 3 if cols % (3 * 128) == 0 else 1
    rows = cols // pieces

    def kernel(pos, x_hbm, we_hbm, b_hbm, wd_hbm, pre_ref, act_ref, act_t_ref, *refs):
        out_refs, (w_ref, x_ref, we_ref, b_ref, sems, w_sems) = refs[: len(jobs)], refs[len(jobs):]
        loads = [pltpu.make_async_copy(b_hbm, b_ref, sems.at[0])]
        for i in range(pieces):
            span = pl.ds(i * rows, rows)
            loads.append(pltpu.make_async_copy(x_hbm.at[:, span], x_ref.at[:, span], sems.at[2 * i + 1]))
            loads.append(pltpu.make_async_copy(we_hbm.at[span], we_ref.at[span], sems.at[2 * i + 2]))
        for load in loads:
            load.start()
        copies, live = weight_copies(pos, jobs, layers, wd_hbm, w_ref, w_sems)
        for copy in copies:
            copy.start()
        loads[0].wait()
        pre = jnp.broadcast_to(b_ref[...], (toks, width))
        for i in range(pieces):
            loads[2 * i + 1].wait()
            loads[2 * i + 2].wait()
            span = pl.ds(i * rows, rows)
            pre += jnp.dot(x_ref[:, span], we_ref[span], preferred_element_type=F32)
        pre_ref[...] = pre
        act = jnp.maximum(pre, 0.0).astype(BF16)
        act_ref[...] = act
        partial_sums(copies, live, act, w_ref, out_refs)
        act_t_ref[...] = act.T

    out = pl.pallas_call(
        kernel,
        in_specs=[IN_SMEM] + [IN_PLACE] * 4,
        out_specs=[IN_VMEM] * (3 + len(jobs)),
        out_shape=[
            pltpu.VMEM((toks, width), F32),
            pltpu.VMEM((toks, width), BF16),
            pltpu.VMEM((width, toks), BF16),
        ]
        + job_shapes(jobs, toks, half),
        scratch_shapes=[
            pltpu.VMEM((len(jobs), width, half), BF16),
            pltpu.VMEM(x.shape, BF16),
            pltpu.VMEM(w_enc.shape, BF16),
            pltpu.VMEM(b_enc.shape, F32),
            pltpu.SemaphoreType.DMA((2 * pieces + 1,)),
            pltpu.SemaphoreType.DMA((len(jobs),)),
        ],
        **params(),
    )(pos, in_hbm(x), in_hbm(w_enc), in_hbm(b_enc), in_hbm(w_dec))
    return out[0], out[1], out[2], dict(zip(jobs, out[3:]))


def decode(pos, act, w_dec, jobs):
    layers, width, cols = w_dec.shape
    toks, half = act.shape[0], cols // 2

    def kernel(pos, act_ref, wd_hbm, *refs):
        out_refs, (w_ref, w_sems) = refs[: len(jobs)], refs[len(jobs):]
        copies, live = weight_copies(pos, jobs, layers, wd_hbm, w_ref, w_sems)
        for copy in copies:
            copy.start()
        partial_sums(copies, live, act_ref[...], w_ref, out_refs)

    out = pl.pallas_call(
        kernel,
        in_specs=[IN_SMEM, IN_VMEM, IN_PLACE],
        out_specs=[IN_VMEM] * len(jobs),
        out_shape=job_shapes(jobs, toks, half),
        scratch_shapes=[
            pltpu.VMEM((len(jobs), width, half), BF16),
            pltpu.SemaphoreType.DMA((len(jobs),)),
        ],
        **params(),
    )(pos, in_vmem(act), in_hbm(w_dec))
    return dict(zip(jobs, out))


def backward(pos, jobs, errs, act_t, w_dec, carry, weights=None, ahead=(), last=None, cost=1):
    layers, width, cols = w_dec.shape
    toks, half = errs[0].shape
    bits = layers.bit_length() - 1
    scale = toks ** (-0.5)
    count = len(jobs)
    pieces = 3 if cols % (3 * 128) == 0 else 1

    def kernel(pos, *refs):
        refs = list(refs)
        take = lambda n: [refs.pop(0) for _ in range(n)]
        err_refs, (act_t_ref, wd_hbm) = take(count), take(2)
        old_ref = take(2)[0] if carry is not None else None
        w_refs = take(count) if weights is not None else None
        x_ref, pre_ref = take(2) if last is not None else (None, None)
        sum_ref, grad_hbm = take(2)
        ahead_refs = take(len(ahead))
        genc_hbm, gb_ref = take(2) if last is not None else (None, None)
        grad_ref, grad_sems = take(2)
        load_ref, load_sems = take(2) if weights is None else (None, None)
        ahead_sems = take(1)[0] if ahead else None
        genc_ref, enc_sems = take(2) if last is not None else (None, None)

        def place(slot, part):
            side = pos[1] if part == 0 else 1 - pos[1]
            target = pos[0] ^ slot_offset(slot, side, bits)
            return target, pl.ds(pl.multiple_of(side * half, half), half)

        loads, writes, live, later = [], [], [], []
        for i, job in enumerate(jobs):
            target, span = place(*job)
            live.append(target >= pos[0])
            writes.append(pltpu.make_async_copy(grad_ref.at[i], grad_hbm.at[target, :, span], grad_sems.at[i]))
            if weights is None:
                loads.append(pltpu.make_async_copy(wd_hbm.at[target, :, span], load_ref.at[i], load_sems.at[i]))
        for i, job in enumerate(ahead):
            target, span = place(*job)
            later.append(pltpu.make_async_copy(wd_hbm.at[target, :, span], ahead_refs[i], ahead_sems.at[i]))
        for copy in loads + later:
            copy.start()
        if weights is None:
            w_refs = [load_ref.at[i] for i in range(count)]

        sum_ref[...] = jnp.zeros_like(sum_ref) if carry is None else old_ref[...]
        for i in range(count):

            @pl.when(live[i])
            def _():
                grad = jnp.dot(act_t_ref[...], err_refs[i][...], preferred_element_type=F32)
                grad_ref[i] = (grad * scale).astype(BF16)

            @pl.when(jnp.logical_not(live[i]))
            def _():
                grad_ref[i] = jnp.zeros((width, half), BF16)

            writes[i].start()
        for i in range(count):
            if weights is None:
                loads[i].wait()

            @pl.when(live[i])
            def _():
                sum_ref[...] += lax.dot_general(
                    err_refs[i][...], w_refs[i][...], (((1,), (1,)), ((), ())), preferred_element_type=F32
                )

        if last is not None:
            pre_grad = jnp.where(pre_ref[...] > 0, sum_ref[...] * scale, 0.0).astype(BF16)
            gb_ref[...] = jnp.sum(pre_grad.astype(F32), axis=0, keepdims=True)
            for i in range(pieces):
                span = pl.ds(i * (cols // pieces), cols // pieces)
                genc_ref[span] = lax.dot_general(
                    x_ref[:, span], pre_grad, (((0,), (0,)), ((), ())), preferred_element_type=F32
                ).astype(BF16)
                write = pltpu.make_async_copy(genc_ref.at[span], genc_hbm.at[span], enc_sems.at[i])
                write.start()
                writes.append(write)
        for copy in later + writes:
            copy.wait()

    in_specs = [IN_SMEM] + [IN_VMEM] * (count + 1) + [IN_PLACE]
    args = [pos] + [in_vmem(a) for a in (*errs, act_t)] + [in_hbm(w_dec)]
    out_specs = [IN_VMEM, IN_PLACE] + [IN_VMEM] * len(ahead)
    out_shape = [pltpu.VMEM((toks, width), F32), pltpu.HBM((layers, width, cols), BF16)]
    out_shape += [pltpu.VMEM((width, half), BF16)] * len(ahead)
    scratch = [pltpu.VMEM((count, width, half), BF16), pltpu.SemaphoreType.DMA((count,))]
    aliases = {}
    if carry is not None:
        in_specs += [IN_VMEM, IN_PLACE]
        args += [in_vmem(carry[0]), carry[1]]
        aliases = {len(args) - 1: 1}
    if weights is None:
        scratch += [pltpu.VMEM((count, width, half), BF16), pltpu.SemaphoreType.DMA((count,))]
    else:
        in_specs += [IN_VMEM] * count
        args += [in_vmem(a) for a in weights]
    if ahead:
        scratch += [pltpu.SemaphoreType.DMA((len(ahead),))]
    if last is not None:
        in_specs += [IN_VMEM] * 2
        args += [in_vmem(a) for a in last]
        out_specs += [IN_PLACE, IN_VMEM]
        out_shape += [pltpu.HBM((cols, width), BF16), jax.ShapeDtypeStruct((1, width), F32)]
        scratch += [pltpu.VMEM((cols, width), BF16), pltpu.SemaphoreType.DMA((pieces,))]
    return pl.pallas_call(
        kernel,
        in_specs=in_specs,
        out_specs=out_specs,
        out_shape=out_shape,
        scratch_shapes=scratch,
        input_output_aliases=aliases,
        **params(cost),
    )(*args)


def add_up(values, dtype, cost=1):
    def kernel(*refs):
        total = refs[0][...].astype(F32)
        for ref in refs[1:-1]:
            total += ref[...].astype(F32)
        refs[-1][...] = total.astype(dtype)

    return pl.pallas_call(
        kernel,
        in_specs=[IN_VMEM] * len(values),
        out_specs=IN_VMEM,
        out_shape=pltpu.VMEM(values[0].shape, dtype),
        **params(cost),
    )(*[in_vmem(v) for v in values])


def add_rows(high, parts, whole, pieces, dtype):
    n, cols = whole[0].shape[0] // 2, whole[0].shape[1]

    def kernel(high, *refs):
        rest = list(refs[len(whole):])
        for i, part in enumerate(parts):
            start = (high[0] if part == 0 else 1 - high[0]) * n
            total = jnp.zeros((n, cols), F32)
            for ref in refs[: len(whole)]:
                total += ref[pl.ds(pl.multiple_of(start, n), n)].astype(F32)
            for _ in pieces[i]:
                total += rest.pop(0)[...].astype(F32)
            refs[i - len(parts)][...] = total.astype(dtype)

    values = [*whole, *[p for group in pieces for p in group]]
    return pl.pallas_call(
        kernel,
        in_specs=[IN_SMEM] + [IN_VMEM] * len(values),
        out_specs=[IN_VMEM] * len(parts),
        out_shape=[pltpu.VMEM((n, cols), dtype)] * len(parts),
        **params(),
    )(high, *[in_vmem(v) for v in values])


def join_rows(high, kept, far, cost=1):
    n, cols = kept.shape

    def kernel(high, kept_ref, far_ref, out_ref):
        out_ref[pl.ds(pl.multiple_of(high[0] * n, n), n)] = kept_ref[...]
        out_ref[pl.ds(pl.multiple_of((1 - high[0]) * n, n), n)] = far_ref[...]

    return pl.pallas_call(
        kernel,
        in_specs=[IN_SMEM] + [IN_VMEM] * 2,
        out_specs=IN_VMEM,
        out_shape=pltpu.VMEM((2 * n, cols), kept.dtype),
        **params(cost),
    )(high, in_vmem(kept), in_vmem(far))


def shards(inputs, targets, w_enc, b_enc, w_dec):
    layers, cols = w_dec.shape[1], w_dec.shape[3]
    feats = lax.axis_size("feat")
    bits, feat_bits = layers.bit_length() - 1, feats.bit_length() - 1
    half = cols // 2
    own_layer, own_feat = lax.axis_index("layer"), lax.axis_index("feat")
    core = own_feat & 1
    pos = jnp.stack([own_layer, core]).astype(jnp.int32)
    x, tgt, wd = inputs[0], targets[0], w_dec[0]

    def swap_feat(value, bit):
        return lax.ppermute(value, "feat", [(f, f ^ (1 << bit)) for f in range(feats)])

    def swap_layer(value, step, cross=False):
        pairs = [
            (l * feats + f, (l ^ (1 << layer_bit(step, f & 1, bits))) * feats + (f ^ 2 if cross else f))
            for l in range(layers)
            for f in range(feats)
        ]
        return lax.ppermute(value, ("layer", "feat"), pairs)

    def jobs(low, high):
        return [(s, part) for s in reversed(range(low, high)) for part in (1, 0)]

    mid, final = layers // 2, layers - 1
    high = ((own_feat >> 1) & 1).reshape(1)
    pre, act, act_t, sums = encode(pos, x, w_enc[0], b_enc, wd, [(final, 1)])
    got = {final: swap_feat(sums[final, 1], 0)}
    sums |= decode(pos, act, wd, [(final, 0)] + [(s, 1) for s in reversed(range(mid, final))])
    for s in reversed(range(mid, final)):
        got[s] = swap_feat(sums[s, 1], 0)
    away = add_up([sums[final, 0], got[final]], BF16)
    slots = [[] for _ in range(mid)]
    slots[final - mid].append(swap_layer(away, 0))
    sums |= decode(pos, after(act, away), wd, [(s, 0) for s in reversed(range(mid, final))] + jobs(0, mid))
    for s in reversed(range(mid)):
        got[s] = swap_feat(sums[s, 1], 0)
        slots[s] += [sums[s, 0], got[s]]
    for s in range(mid, final):
        slots.append([after(sums[s, 0], sums[0, 0]), got[s]])
    tgt = after(tgt, away)
    rows = []
    for step in range(bits):
        n = layers >> (step + 1)
        for s in reversed(range(n)):
            if step == 0 and n + s == final:
                continue
            if s > 0:
                slots[s].append(swap_layer(add_up(slots[n + s], BF16), step))
            else:
                kept, away = add_rows(high, (0, 1), slots[n], ([], []), BF16)
                rows += [swap_layer(kept, step), swap_layer(away, step, cross=True)]

    pair_tgt = swap_feat(tgt, 0)
    pair = jnp.where(core == 0, jnp.stack([tgt, pair_tgt]), jnp.stack([pair_tgt, tgt]))
    pair = -jnp.concatenate([pair[0], pair[1]], axis=1)
    span = pair.shape[1]
    chip, chips = own_feat >> 1, feats // 2
    spread = jnp.zeros((x.shape[0], half), BF16)
    for i in range(chips // 2):
        padded = jnp.pad(pair, ((0, 0), (i * span, half - (i + 1) * span)))
        spread = jnp.where(chip == core * (chips // 2) + i, padded, spread)

    (away,) = add_rows(high, (1,), [*slots[0], spread], ([],), BF16)
    rows.append(swap_feat(away, 1))
    (rows,) = add_rows(high, (0,), [*slots[0], spread], (rows,), F32)
    for bit in range(2, feat_bits - 1):
        n = rows.shape[0] // 2
        upper = ((own_feat >> bit) & 1) == 1
        away = jnp.where(upper, rows[:n], rows[n:]).astype(BF16)
        rows = jnp.where(upper, rows[n:], rows[:n]) + swap_feat(away, bit).astype(F32)
    rows = rows + swap_feat(rows.astype(BF16), feat_bits - 1).astype(F32)
    err = rows.astype(BF16)
    for bit in reversed(range(2, feat_bits - 1)):
        upper = ((own_feat >> bit) & 1) == 1
        far = swap_feat(err, bit)
        err = jnp.concatenate([jnp.where(upper, far, err), jnp.where(upper, err, far)])

    near = [swap_layer(err, step) for step in reversed(range(bits))]
    cross = swap_layer(err, bits - 1, cross=True)
    far = swap_feat(err, 1)
    slots = [join_rows(high, err, far)]
    start = backward(pos, [(0, 0)], [slots[0]], act_t, wd, None)
    for i, step in enumerate(reversed(range(bits))):
        for s in range(len(slots)):
            if s > 0:
                slots.append(swap_layer(slots[s], step))
            elif i > 0:
                slots.append(join_rows(high, near[i], swap_layer(far, step)))
            else:
                slots.append(join_rows(high, near[i], after(cross, start[0]), 1))
    middle = [(0, 1)] + [(s, part) for s in range(1, final) for part in (0, 1)]
    errs = [slots[s] if part == 0 else swap_feat(slots[0] if s == 0 else slots[s], 0) for s, part in middle]
    *carry, w_own, w_other = backward(pos, middle, errs, act_t, wd, start, ahead=[(final, 0), (final, 1)])
    own = add_up([after(slots[final], carry[0])], BF16, 100000000000)
    other = swap_feat(own, 0)
    carry = backward(pos, [(final, 0)], [own], act_t, wd, carry, [w_own])
    carry = backward(pos, [(final, 1)], [other], act_t, wd, carry, [w_other], last=(x, pre))
    act_sum, grad_dec, grad_enc, grad_benc = carry
    return grad_enc[None], grad_dec[None], grad_benc


def solution(mesh):
    in_specs = (
        P("layer", None, None),
        P("layer", None, "feat"),
        P("layer", None, "feat"),
        P("layer", "feat"),
        P("layer", None, "feat", None),
    )
    out_specs = (P("layer", None, "feat"), P("layer", None, "feat", None), P("layer", "feat"))
    return jax.shard_map(shards, mesh=mesh, in_specs=in_specs, out_specs=out_specs, check_vma=False)
```

```python
import jax
import jax.numpy as jnp
from jax import lax
from jax.experimental import pallas as pl
from jax.experimental.pallas import tpu as pltpu
from jax.sharding import PartitionSpec as P

F32 = jnp.float32
BF16 = jnp.bfloat16
VMEM_LIMIT = 16 * 1024 * 1024
IN_VMEM = pl.BlockSpec(memory_space=pltpu.VMEM)
IN_PLACE = pl.BlockSpec(memory_space=pl.ANY)
IN_SMEM = pl.BlockSpec(memory_space=pltpu.SMEM)


def slot_offset(slot, core, bits):
    mirrored = 0
    for k in range(bits):
        mirrored = mirrored | (((slot >> k) & 1) << (bits - 1 - k))
    return jnp.where(core == 1, slot, mirrored)


def layer_bit(step, core, bits):
    return bits - 1 - step if core == 1 else step


def params(cost=1):
    return dict(
        compiler_params=pltpu.CompilerParams(vmem_limit_bytes=VMEM_LIMIT),
        cost_estimate=pl.CostEstimate(flops=cost, bytes_accessed=1, transcendentals=0),
    )


def in_hbm(value):
    return pltpu.with_memory_space_constraint(value, pltpu.HBM)


def in_vmem(value):
    return pltpu.with_memory_space_constraint(value, pltpu.VMEM)


def after(value, *others):
    return lax.optimization_barrier((value, *others))[0]


def weight_copies(pos, jobs, layers, wd_hbm, w_ref, sems):
    half = w_ref.shape[-1]
    bits = layers.bit_length() - 1
    copies, live = [], []
    for i, (slot, part) in enumerate(jobs):
        side = (pos[0] & 1) if part == 0 else 1 - (pos[0] & 1)
        target = (pos[0] >> 1) ^ slot_offset(slot, side, bits)
        cols = pl.ds(pl.multiple_of(side * half, half), half)
        copies.append(pltpu.make_async_copy(wd_hbm.at[target, :, cols], w_ref.at[i], sems.at[i]))
        live.append(target >= (pos[0] >> 1))
    return copies, live


def partial_sums(copies, live, act, w_ref, out_refs):
    for i, out_ref in enumerate(out_refs):
        copies[i].wait()

        @pl.when(live[i])
        def _():
            out_ref[...] = jnp.dot(act, w_ref[i], preferred_element_type=F32).astype(out_ref.dtype)

        @pl.when(jnp.logical_not(live[i]))
        def _():
            out_ref[...] = jnp.zeros_like(out_ref)


def job_shapes(jobs, toks, half):
    return [pltpu.VMEM((toks, half), F32 if part == 0 else BF16) for _, part in jobs]


def encode(pos, x, w_enc, b_enc, w_dec, jobs):
    layers, width, cols = w_dec.shape
    toks, half = x.shape[0], cols // 2
    pieces = 3 if cols % (3 * 128) == 0 else 1
    rows = cols // pieces

    def kernel(pos, x_hbm, we_hbm, b_hbm, wd_hbm, pre_ref, act_ref, act_t_ref, *refs):
        out_refs, (w_ref, x_ref, we_ref, b_ref, sems, w_sems) = refs[: len(jobs)], refs[len(jobs):]
        loads = [pltpu.make_async_copy(b_hbm, b_ref, sems.at[0])]
        for i in range(pieces):
            span = pl.ds(i * rows, rows)
            loads.append(pltpu.make_async_copy(x_hbm.at[:, span], x_ref.at[:, span], sems.at[2 * i + 1]))
            loads.append(pltpu.make_async_copy(we_hbm.at[span], we_ref.at[span], sems.at[2 * i + 2]))
        for load in loads:
            load.start()
        copies, live = weight_copies(pos, jobs, layers, wd_hbm, w_ref, w_sems)
        for copy in copies:
            copy.start()
        loads[0].wait()
        pre = jnp.broadcast_to(b_ref[...], (toks, width))
        for i in range(pieces):
            loads[2 * i + 1].wait()
            loads[2 * i + 2].wait()
            span = pl.ds(i * rows, rows)
            pre += jnp.dot(x_ref[:, span], we_ref[span], preferred_element_type=F32)
        pre_ref[...] = pre
        act = jnp.maximum(pre, 0.0).astype(BF16)
        act_ref[...] = act
        partial_sums(copies, live, act, w_ref, out_refs)
        act_t_ref[...] = act.T

    out = pl.pallas_call(
        kernel,
        in_specs=[IN_SMEM] + [IN_PLACE] * 4,
        out_specs=[IN_VMEM] * (3 + len(jobs)),
        out_shape=[
            pltpu.VMEM((toks, width), F32),
            pltpu.VMEM((toks, width), BF16),
            pltpu.VMEM((width, toks), BF16),
        ]
        + job_shapes(jobs, toks, half),
        scratch_shapes=[
            pltpu.VMEM((len(jobs), width, half), BF16),
            pltpu.VMEM(x.shape, BF16),
            pltpu.VMEM(w_enc.shape, BF16),
            pltpu.VMEM(b_enc.shape, F32),
            pltpu.SemaphoreType.DMA((2 * pieces + 1,)),
            pltpu.SemaphoreType.DMA((len(jobs),)),
        ],
        **params(),
    )(pos, in_hbm(x), in_hbm(w_enc), in_hbm(b_enc), in_hbm(w_dec))
    return out[0], out[1], out[2], dict(zip(jobs, out[3:]))


def decode(pos, act, w_dec, jobs):
    layers, width, cols = w_dec.shape
    toks, half = act.shape[0], cols // 2

    def kernel(pos, act_ref, wd_hbm, *refs):
        out_refs, (w_ref, w_sems) = refs[: len(jobs)], refs[len(jobs):]
        copies, live = weight_copies(pos, jobs, layers, wd_hbm, w_ref, w_sems)
        for copy in copies:
            copy.start()
        partial_sums(copies, live, act_ref[...], w_ref, out_refs)

    out = pl.pallas_call(
        kernel,
        in_specs=[IN_SMEM, IN_VMEM, IN_PLACE],
        out_specs=[IN_VMEM] * len(jobs),
        out_shape=job_shapes(jobs, toks, half),
        scratch_shapes=[
            pltpu.VMEM((len(jobs), width, half), BF16),
            pltpu.SemaphoreType.DMA((len(jobs),)),
        ],
        **params(),
    )(pos, in_vmem(act), in_hbm(w_dec))
    return dict(zip(jobs, out))


def backward(pos, jobs, errs, act_t, w_dec, carry, weights=None, ahead=(), last=None, cost=1):
    layers, width, cols = w_dec.shape
    toks, half = errs[0].shape
    bits = layers.bit_length() - 1
    scale = toks ** (-0.5)
    count = len(jobs)
    pieces = 3 if cols % (3 * 128) == 0 else 1

    def kernel(pos, *refs):
        refs = list(refs)
        take = lambda n: [refs.pop(0) for _ in range(n)]
        err_refs, (act_t_ref, wd_hbm) = take(count), take(2)
        old_ref = take(2)[0] if carry is not None else None
        w_refs = take(count) if weights is not None else None
        x_ref, pre_ref = take(2) if last is not None else (None, None)
        sum_ref = take(1)[0] if last is None else None
        grad_hbm = take(1)[0]
        ahead_refs = take(len(ahead))
        genc_hbm, gb_hbm = take(2) if last is not None else (None, None)
        grad_ref, grad_sems = take(2)
        load_ref, load_sems = take(2) if weights is None else (None, None)
        ahead_sems = take(1)[0] if ahead else None
        genc_ref, gb_ref, total_ref, enc_sems = take(4) if last is not None else (None,) * 4

        def place(slot, part):
            side = (pos[0] & 1) if part == 0 else 1 - (pos[0] & 1)
            target = (pos[0] >> 1) ^ slot_offset(slot, side, bits)
            return target, pl.ds(pl.multiple_of(side * half, half), half)

        loads, writes, live, later = [], [], [], []
        for i, job in enumerate(jobs):
            target, span = place(*job)
            live.append(target >= (pos[0] >> 1))
            writes.append(pltpu.make_async_copy(grad_ref.at[i], grad_hbm.at[target, :, span], grad_sems.at[i]))
            if weights is None:
                loads.append(pltpu.make_async_copy(wd_hbm.at[target, :, span], load_ref.at[i], load_sems.at[i]))
        for i, job in enumerate(ahead):
            target, span = place(*job)
            later.append(pltpu.make_async_copy(wd_hbm.at[target, :, span], ahead_refs[i], ahead_sems.at[i]))
        for copy in loads + later:
            copy.start()
        if weights is None:
            w_refs = [load_ref.at[i] for i in range(count)]

        if last is not None:
            sum_ref = total_ref
        sum_ref[...] = jnp.zeros_like(sum_ref) if carry is None else old_ref[...]
        for i in range(count):

            @pl.when(live[i])
            def _():
                grad = jnp.dot(act_t_ref[...], err_refs[i][...], preferred_element_type=F32)
                grad_ref[i] = (grad * scale).astype(BF16)

            @pl.when(jnp.logical_not(live[i]))
            def _():
                grad_ref[i] = jnp.zeros((width, half), BF16)

            writes[i].start()
        for i in range(count):
            if weights is None:
                loads[i].wait()

            @pl.when(live[i])
            def _():
                sum_ref[...] += lax.dot_general(
                    err_refs[i][...], w_refs[i][...], (((1,), (1,)), ((), ())), preferred_element_type=F32
                )

        if last is not None:
            pre_grad = jnp.where(pre_ref[...] > 0, sum_ref[...] * scale, 0.0).astype(BF16)
            gb_ref[...] = jnp.sum(pre_grad.astype(F32), axis=0, keepdims=True)
            writes.append(pltpu.make_async_copy(gb_ref, gb_hbm, enc_sems.at[pieces]))
            writes[-1].start()
            for i in range(pieces):
                span = pl.ds(i * (cols // pieces), cols // pieces)
                genc_ref[span] = lax.dot_general(
                    x_ref[:, span], pre_grad, (((0,), (0,)), ((), ())), preferred_element_type=F32
                ).astype(BF16)
                write = pltpu.make_async_copy(genc_ref.at[span], genc_hbm.at[span], enc_sems.at[i])
                write.start()
                writes.append(write)
        for copy in later + writes:
            copy.wait()

    in_specs = [IN_SMEM] + [IN_VMEM] * (count + 1) + [IN_PLACE]
    args = [pos] + [in_vmem(a) for a in (*errs, act_t)] + [in_hbm(w_dec)]
    sums = 0 if last is not None else 1
    out_specs = [IN_VMEM] * sums + [IN_PLACE] + [IN_VMEM] * len(ahead)
    out_shape = [pltpu.VMEM((toks, width), F32)] * sums + [pltpu.HBM((layers, width, cols), BF16)]
    out_shape += [pltpu.VMEM((width, half), BF16)] * len(ahead)
    scratch = [pltpu.VMEM((count, width, half), BF16), pltpu.SemaphoreType.DMA((count,))]
    aliases = {}
    if carry is not None:
        in_specs += [IN_VMEM, IN_PLACE]
        args += [in_vmem(carry[0]), carry[1]]
        aliases = {len(args) - 1: sums}
    if weights is None:
        scratch += [pltpu.VMEM((count, width, half), BF16), pltpu.SemaphoreType.DMA((count,))]
    else:
        in_specs += [IN_VMEM] * count
        args += [in_vmem(a) for a in weights]
    if ahead:
        scratch += [pltpu.SemaphoreType.DMA((len(ahead),))]
    if last is not None:
        in_specs += [IN_VMEM] * 2
        args += [in_vmem(a) for a in last]
        out_specs += [IN_PLACE] * 2
        out_shape += [pltpu.HBM((cols, width), BF16), pltpu.HBM((1, width), F32)]
        scratch += [
            pltpu.VMEM((cols, width), BF16),
            pltpu.VMEM((1, width), F32),
            pltpu.VMEM((toks, width), F32),
            pltpu.SemaphoreType.DMA((pieces + 1,)),
        ]
    return pl.pallas_call(
        kernel,
        in_specs=in_specs,
        out_specs=out_specs,
        out_shape=out_shape,
        scratch_shapes=scratch,
        input_output_aliases=aliases,
        **params(cost),
    )(*args)


def add_up(values, dtype, cost=1):
    def kernel(*refs):
        total = refs[0][...].astype(F32)
        for ref in refs[1:-1]:
            total += ref[...].astype(F32)
        refs[-1][...] = total.astype(dtype)

    return pl.pallas_call(
        kernel,
        in_specs=[IN_VMEM] * len(values),
        out_specs=IN_VMEM,
        out_shape=pltpu.VMEM(values[0].shape, dtype),
        **params(cost),
    )(*[in_vmem(v) for v in values])


def add_rows(high, parts, whole, pieces, dtype):
    n, cols = whole[0].shape[0] // 2, whole[0].shape[1]

    def kernel(high, *refs):
        rest = list(refs[len(whole):])
        for i, part in enumerate(parts):
            start = (high[0] if part == 0 else 1 - high[0]) * n
            total = jnp.zeros((n, cols), F32)
            for ref in refs[: len(whole)]:
                total += ref[pl.ds(pl.multiple_of(start, n), n)].astype(F32)
            for _ in pieces[i]:
                total += rest.pop(0)[...].astype(F32)
            refs[i - len(parts)][...] = total.astype(dtype)

    values = [*whole, *[p for group in pieces for p in group]]
    return pl.pallas_call(
        kernel,
        in_specs=[IN_SMEM] + [IN_VMEM] * len(values),
        out_specs=[IN_VMEM] * len(parts),
        out_shape=[pltpu.VMEM((n, cols), dtype)] * len(parts),
        **params(),
    )(high, *[in_vmem(v) for v in values])


def join_rows(high, kept, far, cost=1):
    n, cols = kept.shape

    def kernel(high, kept_ref, far_ref, out_ref):
        out_ref[pl.ds(pl.multiple_of(high[0] * n, n), n)] = kept_ref[...]
        out_ref[pl.ds(pl.multiple_of((1 - high[0]) * n, n), n)] = far_ref[...]

    return pl.pallas_call(
        kernel,
        in_specs=[IN_SMEM] + [IN_VMEM] * 2,
        out_specs=IN_VMEM,
        out_shape=pltpu.VMEM((2 * n, cols), kept.dtype),
        **params(cost),
    )(high, in_vmem(kept), in_vmem(far))


def shards(inputs, targets, w_enc, b_enc, w_dec):
    layers, cols = w_dec.shape[1], w_dec.shape[3]
    feats = lax.axis_size("feat")
    bits, feat_bits = layers.bit_length() - 1, feats.bit_length() - 1
    half = cols // 2
    own_layer, own_feat = lax.axis_index("layer"), lax.axis_index("feat")
    core = own_feat & 1
    pos = (own_layer * 2 + core).astype(jnp.int32).reshape(1)
    x, tgt, wd = inputs[0], targets[0], w_dec[0]

    def swap_feat(value, bit):
        return lax.ppermute(value, "feat", [(f, f ^ (1 << bit)) for f in range(feats)])

    def swap_layer(value, step, cross=False):
        pairs = [
            (l * feats + f, (l ^ (1 << layer_bit(step, f & 1, bits))) * feats + (f ^ 2 if cross else f))
            for l in range(layers)
            for f in range(feats)
        ]
        return lax.ppermute(value, ("layer", "feat"), pairs)

    def jobs(low, high):
        return [(s, part) for s in reversed(range(low, high)) for part in (1, 0)]

    mid, final = layers // 2, layers - 1
    high = ((own_feat >> 1) & 1).reshape(1)
    pre, act, act_t, sums = encode(pos, x, w_enc[0], b_enc, wd, [(final, 1)])
    got = {final: swap_feat(sums[final, 1], 0)}
    sums |= decode(pos, act, wd, [(final, 0)] + [(s, 1) for s in reversed(range(mid, final))])
    for s in reversed(range(mid, final)):
        got[s] = swap_feat(sums[s, 1], 0)
    away = add_up([sums[final, 0], got[final]], BF16)
    slots = [[] for _ in range(mid)]
    slots[final - mid].append(swap_layer(away, 0))
    sums |= decode(pos, after(act, away), wd, [(s, 0) for s in reversed(range(mid, final))] + jobs(0, mid))
    for s in reversed(range(mid)):
        got[s] = swap_feat(sums[s, 1], 0)
        slots[s] += [sums[s, 0], got[s]]
    for s in range(mid, final):
        slots.append([after(sums[s, 0], sums[0, 0]), got[s]])
    tgt = after(tgt, away)
    rows = []
    for step in range(bits):
        n = layers >> (step + 1)
        for s in reversed(range(n)):
            if step == 0 and n + s == final:
                continue
            if s > 0 or step < bits - 1:
                slots[s].append(swap_layer(add_up(slots[n + s], BF16), step))
            else:
                kept, away = add_rows(high, (0, 1), slots[n], ([], []), BF16)
                rows += [swap_layer(kept, step), add_up([swap_layer(away, step, cross=True)], BF16, 100000000000)]

    pair_tgt = swap_feat(tgt, 0)
    pair = jnp.where(core == 0, jnp.stack([tgt, pair_tgt]), jnp.stack([pair_tgt, tgt]))
    pair = -jnp.concatenate([pair[0], pair[1]], axis=1)
    span = pair.shape[1]
    chip, chips = own_feat >> 1, feats // 2
    spread = jnp.zeros((x.shape[0], half), BF16)
    for i in range(chips // 2):
        padded = jnp.pad(pair, ((0, 0), (i * span, half - (i + 1) * span)))
        spread = jnp.where(chip == core * (chips // 2) + i, padded, spread)

    (away,) = add_rows(high, (1,), [*slots[0], after(spread, kept)], ([],), BF16)
    rows.append(swap_feat(away, 1))
    (rows,) = add_rows(high, (0,), [*slots[0], spread], (rows,), F32)
    for bit in range(2, feat_bits - 1):
        n = rows.shape[0] // 2
        upper = ((own_feat >> bit) & 1) == 1
        away = jnp.where(upper, rows[:n], rows[n:]).astype(BF16)
        rows = jnp.where(upper, rows[n:], rows[:n]) + swap_feat(away, bit).astype(F32)
    rows = rows + swap_feat(rows.astype(BF16), feat_bits - 1).astype(F32)
    err = rows.astype(BF16)
    for bit in reversed(range(2, feat_bits - 1)):
        upper = ((own_feat >> bit) & 1) == 1
        far = swap_feat(err, bit)
        err = jnp.concatenate([jnp.where(upper, far, err), jnp.where(upper, err, far)])

    near = [swap_layer(err, step) for step in reversed(range(bits))]
    cross = swap_layer(err, bits - 1, cross=True)
    far = swap_feat(err, 1)
    slots = [join_rows(high, err, far)]
    start = backward(pos, [(0, 0)], [slots[0]], act_t, wd, None)
    for i, step in enumerate(reversed(range(bits))):
        for s in range(len(slots)):
            if s > 0:
                slots.append(swap_layer(slots[s], step))
            elif i > 0:
                slots.append(join_rows(high, near[i], swap_layer(far, step), 1))
            else:
                slots.append(join_rows(high, near[i], after(cross, start[0]), 1))
    middle = [(0, 1)] + [(s, part) for s in range(1, final) for part in (0, 1)]
    errs = [slots[s] if part == 0 else swap_feat(slots[0] if s == 0 else slots[s], 0) for s, part in middle]
    *carry, w_own, w_other = backward(pos, middle, errs, act_t, wd, start, ahead=[(final, 0), (final, 1)])
    own = add_up([after(slots[final], carry[0])], BF16, 100000000000)
    other = swap_feat(own, 0)
    carry = backward(pos, [(final, 0)], [own], act_t, wd, carry, [w_own])
    carry = backward(pos, [(final, 1)], [other], act_t, wd, carry, [w_other], last=(x, pre))
    grad_dec, grad_enc, grad_benc = carry
    return grad_enc[None], grad_dec[None], grad_benc


def solution(mesh):
    in_specs = (
        P("layer", None, None),
        P("layer", None, "feat"),
        P("layer", None, "feat"),
        P("layer", "feat"),
        P("layer", None, "feat", None),
    )
    out_specs = (P("layer", None, "feat"), P("layer", None, "feat", None), P("layer", "feat"))
    return jax.shard_map(shards, mesh=mesh, in_specs=in_specs, out_specs=out_specs, check_vma=False)
```

```python
import jax
import jax.numpy as jnp
from jax import lax
from jax.experimental import pallas as pl
from jax.experimental.pallas import tpu as pltpu
from jax.sharding import PartitionSpec as P

F32 = jnp.float32
BF16 = jnp.bfloat16
VMEM_LIMIT = 16 * 1024 * 1024
IN_VMEM = pl.BlockSpec(memory_space=pltpu.VMEM)
IN_PLACE = pl.BlockSpec(memory_space=pl.ANY)
IN_SMEM = pl.BlockSpec(memory_space=pltpu.SMEM)


def slot_offset(slot, core, bits):
    mirrored = 0
    for k in range(bits):
        mirrored = mirrored | (((slot >> k) & 1) << (bits - 1 - k))
    return jnp.where(core == 1, slot, mirrored)


def layer_bit(step, core, bits):
    return bits - 1 - step if core == 1 else step


def params(cost=1):
    return dict(
        compiler_params=pltpu.CompilerParams(vmem_limit_bytes=VMEM_LIMIT),
        cost_estimate=pl.CostEstimate(flops=cost, bytes_accessed=1, transcendentals=0),
    )


def in_hbm(value):
    return pltpu.with_memory_space_constraint(value, pltpu.HBM)


def in_vmem(value):
    return pltpu.with_memory_space_constraint(value, pltpu.VMEM)


def after(value, *others):
    return lax.optimization_barrier((value, *others))[0]


def weight_copies(pos, jobs, layers, wd_hbm, w_ref, sems):
    half = w_ref.shape[-1]
    bits = layers.bit_length() - 1
    copies, live = [], []
    for i, (slot, part) in enumerate(jobs):
        side = (pos[0] & 1) if part == 0 else 1 - (pos[0] & 1)
        target = (pos[0] >> 1) ^ slot_offset(slot, side, bits)
        cols = pl.ds(pl.multiple_of(side * half, half), half)
        copies.append(pltpu.make_async_copy(wd_hbm.at[target, :, cols], w_ref.at[i], sems.at[i]))
        live.append(target >= (pos[0] >> 1))
    return copies, live


def partial_sums(copies, live, act, w_ref, out_refs):
    for i, out_ref in enumerate(out_refs):
        copies[i].wait()

        @pl.when(live[i])
        def _():
            out_ref[...] = jnp.dot(act, w_ref[i], preferred_element_type=F32).astype(out_ref.dtype)

        @pl.when(jnp.logical_not(live[i]))
        def _():
            out_ref[...] = jnp.zeros_like(out_ref)


def job_shapes(jobs, toks, half):
    return [pltpu.VMEM((toks, half), F32 if part == 0 else BF16) for _, part in jobs]


def encode(pos, x, w_enc, b_enc, w_dec, jobs):
    layers, width, cols = w_dec.shape
    toks, half = x.shape[0], cols // 2
    pieces = 3 if cols % (3 * 128) == 0 else 1
    rows = cols // pieces

    def kernel(pos, x_hbm, we_hbm, b_hbm, wd_hbm, pre_ref, act_ref, act_t_ref, *refs):
        out_refs, (w_ref, x_ref, we_ref, b_ref, sems, w_sems) = refs[: len(jobs)], refs[len(jobs):]
        loads = [pltpu.make_async_copy(b_hbm, b_ref, sems.at[0])]
        for i in range(pieces):
            span = pl.ds(i * rows, rows)
            loads.append(pltpu.make_async_copy(x_hbm.at[:, span], x_ref.at[:, span], sems.at[2 * i + 1]))
            loads.append(pltpu.make_async_copy(we_hbm.at[span], we_ref.at[span], sems.at[2 * i + 2]))
        for load in loads:
            load.start()
        copies, live = weight_copies(pos, jobs, layers, wd_hbm, w_ref, w_sems)
        for copy in copies:
            copy.start()
        loads[0].wait()
        pre = jnp.broadcast_to(b_ref[...], (toks, width))
        for i in range(pieces):
            loads[2 * i + 1].wait()
            loads[2 * i + 2].wait()
            span = pl.ds(i * rows, rows)
            pre += jnp.dot(x_ref[:, span], we_ref[span], preferred_element_type=F32)
        pre_ref[...] = pre
        act = jnp.maximum(pre, 0.0).astype(BF16)
        act_ref[...] = act
        partial_sums(copies, live, act, w_ref, out_refs)
        act_t_ref[...] = act.T

    out = pl.pallas_call(
        kernel,
        in_specs=[IN_SMEM] + [IN_PLACE] * 4,
        out_specs=[IN_VMEM] * (3 + len(jobs)),
        out_shape=[
            pltpu.VMEM((toks, width), F32),
            pltpu.VMEM((toks, width), BF16),
            pltpu.VMEM((width, toks), BF16),
        ]
        + job_shapes(jobs, toks, half),
        scratch_shapes=[
            pltpu.VMEM((len(jobs), width, half), BF16),
            pltpu.VMEM(x.shape, BF16),
            pltpu.VMEM(w_enc.shape, BF16),
            pltpu.VMEM(b_enc.shape, F32),
            pltpu.SemaphoreType.DMA((2 * pieces + 1,)),
            pltpu.SemaphoreType.DMA((len(jobs),)),
        ],
        **params(),
    )(pos, in_hbm(x), in_hbm(w_enc), in_hbm(b_enc), in_hbm(w_dec))
    return out[0], out[1], out[2], dict(zip(jobs, out[3:]))


def decode(pos, act, w_dec, jobs):
    layers, width, cols = w_dec.shape
    toks, half = act.shape[0], cols // 2

    def kernel(pos, act_ref, wd_hbm, *refs):
        out_refs, (w_ref, w_sems) = refs[: len(jobs)], refs[len(jobs):]
        copies, live = weight_copies(pos, jobs, layers, wd_hbm, w_ref, w_sems)
        for copy in copies:
            copy.start()
        partial_sums(copies, live, act_ref[...], w_ref, out_refs)

    out = pl.pallas_call(
        kernel,
        in_specs=[IN_SMEM, IN_VMEM, IN_PLACE],
        out_specs=[IN_VMEM] * len(jobs),
        out_shape=job_shapes(jobs, toks, half),
        scratch_shapes=[
            pltpu.VMEM((len(jobs), width, half), BF16),
            pltpu.SemaphoreType.DMA((len(jobs),)),
        ],
        **params(),
    )(pos, in_vmem(act), in_hbm(w_dec))
    return dict(zip(jobs, out))


def backward(pos, jobs, errs, act_t, w_dec, carry, weights=None, ahead=(), last=None, cost=1):
    layers, width, cols = w_dec.shape
    toks, half = errs[0].shape
    bits = layers.bit_length() - 1
    scale = toks ** (-0.5)
    count = len(jobs)
    pieces = 3 if cols % (3 * 128) == 0 else 1

    def kernel(pos, *refs):
        refs = list(refs)
        take = lambda n: [refs.pop(0) for _ in range(n)]
        err_refs, (act_t_ref, wd_hbm) = take(count), take(2)
        old_ref = take(2)[0] if carry is not None else None
        w_refs = take(count) if weights is not None else None
        x_ref, pre_ref = take(2) if last is not None else (None, None)
        sum_ref = take(1)[0] if last is None else None
        grad_hbm = take(1)[0]
        ahead_refs = take(len(ahead))
        genc_hbm, gb_hbm = take(2) if last is not None else (None, None)
        grad_ref, grad_sems = take(2)
        load_ref, load_sems = take(2) if weights is None else (None, None)
        ahead_sems = take(1)[0] if ahead else None
        genc_ref, gb_ref, total_ref, enc_sems = take(4) if last is not None else (None,) * 4

        def place(slot, part):
            side = (pos[0] & 1) if part == 0 else 1 - (pos[0] & 1)
            target = (pos[0] >> 1) ^ slot_offset(slot, side, bits)
            return target, pl.ds(pl.multiple_of(side * half, half), half)

        loads, writes, live, later = [], [], [], []
        for i, job in enumerate(jobs):
            target, span = place(*job)
            live.append(target >= (pos[0] >> 1))
            writes.append(pltpu.make_async_copy(grad_ref.at[i], grad_hbm.at[target, :, span], grad_sems.at[i]))
            if weights is None:
                loads.append(pltpu.make_async_copy(wd_hbm.at[target, :, span], load_ref.at[i], load_sems.at[i]))
        for i, job in enumerate(ahead):
            target, span = place(*job)
            later.append(pltpu.make_async_copy(wd_hbm.at[target, :, span], ahead_refs[i], ahead_sems.at[i]))
        for copy in loads + later:
            copy.start()
        if weights is None:
            w_refs = [load_ref.at[i] for i in range(count)]

        if last is not None:
            sum_ref = total_ref
        sum_ref[...] = jnp.zeros_like(sum_ref) if carry is None else old_ref[...]
        for i in range(count):

            @pl.when(live[i])
            def _():
                grad = jnp.dot(act_t_ref[...], err_refs[i][...], preferred_element_type=F32)
                grad_ref[i] = (grad * scale).astype(BF16)

            @pl.when(jnp.logical_not(live[i]))
            def _():
                grad_ref[i] = jnp.zeros((width, half), BF16)

            writes[i].start()
        for i in range(count):
            if weights is None:
                loads[i].wait()

            @pl.when(live[i])
            def _():
                sum_ref[...] += lax.dot_general(
                    err_refs[i][...], w_refs[i][...], (((1,), (1,)), ((), ())), preferred_element_type=F32
                )

        if last is not None:
            pre_grad = jnp.where(pre_ref[...] > 0, sum_ref[...] * scale, 0.0).astype(BF16)
            gb_ref[...] = jnp.sum(pre_grad.astype(F32), axis=0, keepdims=True)
            writes.append(pltpu.make_async_copy(gb_ref, gb_hbm, enc_sems.at[pieces]))
            writes[-1].start()
            for i in range(pieces):
                span = pl.ds(i * (cols // pieces), cols // pieces)
                genc_ref[span] = lax.dot_general(
                    x_ref[:, span], pre_grad, (((0,), (0,)), ((), ())), preferred_element_type=F32
                ).astype(BF16)
                write = pltpu.make_async_copy(genc_ref.at[span], genc_hbm.at[span], enc_sems.at[i])
                write.start()
                writes.append(write)
        for copy in later + writes:
            copy.wait()

    in_specs = [IN_SMEM] + [IN_VMEM] * (count + 1) + [IN_PLACE]
    args = [pos] + [in_vmem(a) for a in (*errs, act_t)] + [in_hbm(w_dec)]
    sums = 0 if last is not None else 1
    out_specs = [IN_VMEM] * sums + [IN_PLACE] + [IN_VMEM] * len(ahead)
    out_shape = [pltpu.VMEM((toks, width), F32)] * sums + [pltpu.HBM((layers, width, cols), BF16)]
    out_shape += [pltpu.VMEM((width, half), BF16)] * len(ahead)
    scratch = [pltpu.VMEM((count, width, half), BF16), pltpu.SemaphoreType.DMA((count,))]
    aliases = {}
    if carry is not None:
        in_specs += [IN_VMEM, IN_PLACE]
        args += [in_vmem(carry[0]), carry[1]]
        aliases = {len(args) - 1: sums}
    if weights is None:
        scratch += [pltpu.VMEM((count, width, half), BF16), pltpu.SemaphoreType.DMA((count,))]
    else:
        in_specs += [IN_VMEM] * count
        args += [in_vmem(a) for a in weights]
    if ahead:
        scratch += [pltpu.SemaphoreType.DMA((len(ahead),))]
    if last is not None:
        in_specs += [IN_VMEM] * 2
        args += [in_vmem(a) for a in last]
        out_specs += [IN_PLACE] * 2
        out_shape += [pltpu.HBM((cols, width), BF16), pltpu.HBM((1, width), F32)]
        scratch += [
            pltpu.VMEM((cols, width), BF16),
            pltpu.VMEM((1, width), F32),
            pltpu.VMEM((toks, width), F32),
            pltpu.SemaphoreType.DMA((pieces + 1,)),
        ]
    return pl.pallas_call(
        kernel,
        in_specs=in_specs,
        out_specs=out_specs,
        out_shape=out_shape,
        scratch_shapes=scratch,
        input_output_aliases=aliases,
        **params(cost),
    )(*args)


def add_up(values, dtype, cost=1):
    def kernel(*refs):
        total = refs[0][...].astype(F32)
        for ref in refs[1:-1]:
            total += ref[...].astype(F32)
        refs[-1][...] = total.astype(dtype)

    return pl.pallas_call(
        kernel,
        in_specs=[IN_VMEM] * len(values),
        out_specs=IN_VMEM,
        out_shape=pltpu.VMEM(values[0].shape, dtype),
        **params(cost),
    )(*[in_vmem(v) for v in values])


def add_rows(high, parts, whole, pieces, dtype):
    n, cols = whole[0].shape[0] // 2, whole[0].shape[1]

    def kernel(high, *refs):
        rest = list(refs[len(whole):])
        for i, part in enumerate(parts):
            start = (high[0] if part == 0 else 1 - high[0]) * n
            total = jnp.zeros((n, cols), F32)
            for ref in refs[: len(whole)]:
                total += ref[pl.ds(pl.multiple_of(start, n), n)].astype(F32)
            for _ in pieces[i]:
                total += rest.pop(0)[...].astype(F32)
            refs[i - len(parts)][...] = total.astype(dtype)

    values = [*whole, *[p for group in pieces for p in group]]
    return pl.pallas_call(
        kernel,
        in_specs=[IN_SMEM] + [IN_VMEM] * len(values),
        out_specs=[IN_VMEM] * len(parts),
        out_shape=[pltpu.VMEM((n, cols), dtype)] * len(parts),
        **params(),
    )(high, *[in_vmem(v) for v in values])


def join_rows(high, kept, far, cost=1):
    n, cols = kept.shape

    def kernel(high, kept_ref, far_ref, out_ref):
        out_ref[pl.ds(pl.multiple_of(high[0] * n, n), n)] = kept_ref[...]
        out_ref[pl.ds(pl.multiple_of((1 - high[0]) * n, n), n)] = far_ref[...]

    return pl.pallas_call(
        kernel,
        in_specs=[IN_SMEM] + [IN_VMEM] * 2,
        out_specs=IN_VMEM,
        out_shape=pltpu.VMEM((2 * n, cols), kept.dtype),
        **params(cost),
    )(high, in_vmem(kept), in_vmem(far))


def shards(inputs, targets, w_enc, b_enc, w_dec):
    layers, cols = w_dec.shape[1], w_dec.shape[3]
    feats = lax.axis_size("feat")
    bits, feat_bits = layers.bit_length() - 1, feats.bit_length() - 1
    half = cols // 2
    own_layer, own_feat = lax.axis_index("layer"), lax.axis_index("feat")
    core = own_feat & 1
    pos = (own_layer * 2 + core).astype(jnp.int32).reshape(1)
    x, tgt, wd = inputs[0], targets[0], w_dec[0]

    def swap_feat(value, bit):
        return lax.ppermute(value, "feat", [(f, f ^ (1 << bit)) for f in range(feats)])

    def swap_layer(value, step, cross=False):
        pairs = [
            (l * feats + f, (l ^ (1 << layer_bit(step, f & 1, bits))) * feats + (f ^ 2 if cross else f))
            for l in range(layers)
            for f in range(feats)
        ]
        return lax.ppermute(value, ("layer", "feat"), pairs)

    def jobs(low, high):
        return [(s, part) for s in reversed(range(low, high)) for part in (1, 0)]

    mid, final = layers // 2, layers - 1
    high = ((own_feat >> 1) & 1).reshape(1)
    pre, act, act_t, sums = encode(pos, x, w_enc[0], b_enc, wd, [(final, 1)])
    got = {final: swap_feat(sums[final, 1], 0)}
    sums |= decode(pos, act, wd, [(final, 0)] + [(s, 1) for s in reversed(range(mid, final))])
    for s in reversed(range(mid, final)):
        got[s] = swap_feat(sums[s, 1], 0)
    away = add_up([sums[final, 0], got[final]], BF16)
    slots = [[] for _ in range(mid)]
    slots[final - mid].append(swap_layer(away, 0))
    sums |= decode(pos, after(act, away), wd, [(s, 0) for s in reversed(range(mid, final))] + jobs(0, mid))
    for s in reversed(range(mid)):
        got[s] = swap_feat(sums[s, 1], 0)
        slots[s] += [sums[s, 0], got[s]]
    for s in range(mid, final):
        slots.append([after(sums[s, 0], sums[0, 0]), got[s]])
    tgt = after(tgt, away)
    rows = []
    for step in range(bits):
        n = layers >> (step + 1)
        for s in reversed(range(n)):
            if step == 0 and n + s == final:
                continue
            if s > 0 or step < bits - 1:
                slots[s].append(swap_layer(add_up(slots[n + s], BF16), step))
            else:
                kept, away = add_rows(high, (0, 1), slots[n], ([], []), BF16)
                rows += [swap_layer(kept, step), add_up([swap_layer(away, step, cross=True)], BF16, 100000000000)]

    pair_tgt = swap_feat(tgt, 0)
    pair = jnp.where(core == 0, jnp.stack([tgt, pair_tgt]), jnp.stack([pair_tgt, tgt]))
    pair = -jnp.concatenate([pair[0], pair[1]], axis=1)
    span = pair.shape[1]
    chip, chips = own_feat >> 1, feats // 2
    spread = jnp.zeros((x.shape[0], half), BF16)
    for i in range(chips // 2):
        padded = jnp.pad(pair, ((0, 0), (i * span, half - (i + 1) * span)))
        spread = jnp.where(chip == core * (chips // 2) + i, padded, spread)

    (away,) = add_rows(high, (1,), [*slots[0], after(spread, kept)], ([],), BF16)
    rows.append(swap_feat(away, 1))
    (rows,) = add_rows(high, (0,), [*slots[0], spread], (rows,), F32)
    for bit in range(2, feat_bits - 1):
        n = rows.shape[0] // 2
        upper = ((own_feat >> bit) & 1) == 1
        away = jnp.where(upper, rows[:n], rows[n:]).astype(BF16)
        rows = jnp.where(upper, rows[n:], rows[:n]) + swap_feat(away, bit).astype(F32)
    rows = rows + swap_feat(rows.astype(BF16), feat_bits - 1).astype(F32)
    err = rows.astype(BF16)
    for bit in reversed(range(2, feat_bits - 1)):
        upper = ((own_feat >> bit) & 1) == 1
        far = swap_feat(err, bit)
        err = jnp.concatenate([jnp.where(upper, far, err), jnp.where(upper, err, far)])

    near = [swap_layer(err, step) for step in reversed(range(bits))]
    cross = swap_layer(err, bits - 1, cross=True)
    far = swap_feat(err, 1)
    slots = [join_rows(high, err, far)]
    start = backward(pos, [(0, 0)], [slots[0]], act_t, wd, None)
    for i, step in enumerate(reversed(range(bits))):
        for s in range(len(slots)):
            if s > 0:
                slots.append(swap_layer(slots[s], step))
            elif i > 0:
                slots.append(join_rows(high, near[i], swap_layer(far, step), 10000000000))
            else:
                slots.append(join_rows(high, near[i], after(cross, start[0]), 1))
    between = range(2, final)
    work = [(0, 1), (1, 0), (1, 1)] + [(s, 0) for s in between]
    errs = [swap_feat(slots[0], 0), slots[1], swap_feat(slots[1], 0)] + [slots[s] for s in between]
    others = [swap_feat(slots[s], 0) for s in between]
    rest = [(s, 1) for s in between] + [(final, 0)]
    carry = backward(pos, work, errs, act_t, wd, start, ahead=rest + [(final, 1)])
    carry, w_rest, w_last = carry[:2], carry[2:-1], carry[-1]
    others.append(swap_feat(after(slots[final], carry[0]), 0))
    carry = backward(pos, rest, [*others[:-1], slots[final]], act_t, wd, carry, w_rest)
    carry = backward(pos, [(final, 1)], others[-1:], act_t, wd, carry, [w_last], last=(x, pre))
    grad_dec, grad_enc, grad_benc = carry
    return grad_enc[None], grad_dec[None], grad_benc


def solution(mesh):
    in_specs = (
        P("layer", None, None),
        P("layer", None, "feat"),
        P("layer", None, "feat"),
        P("layer", "feat"),
        P("layer", None, "feat", None),
    )
    out_specs = (P("layer", None, "feat"), P("layer", None, "feat", None), P("layer", "feat"))
    return jax.shard_map(shards, mesh=mesh, in_specs=in_specs, out_specs=out_specs, check_vma=False)
```

```python
import jax
import jax.numpy as jnp
from jax import lax
from jax.experimental import pallas as pl
from jax.experimental.pallas import tpu as pltpu
from jax.sharding import PartitionSpec as P

F32 = jnp.float32
BF16 = jnp.bfloat16
VMEM_LIMIT = 16 * 1024 * 1024
IN_VMEM = pl.BlockSpec(memory_space=pltpu.VMEM)
IN_PLACE = pl.BlockSpec(memory_space=pl.ANY)
IN_SMEM = pl.BlockSpec(memory_space=pltpu.SMEM)


def slot_offset(slot, core, bits):
    mirrored = 0
    for k in range(bits):
        mirrored = mirrored | (((slot >> k) & 1) << (bits - 1 - k))
    return jnp.where(core == 1, slot, mirrored)


def layer_bit(step, core, bits):
    return bits - 1 - step if core == 1 else step


def params(cost=1):
    return dict(
        compiler_params=pltpu.CompilerParams(vmem_limit_bytes=VMEM_LIMIT),
        cost_estimate=pl.CostEstimate(flops=cost, bytes_accessed=1, transcendentals=0),
    )


def in_hbm(value):
    return pltpu.with_memory_space_constraint(value, pltpu.HBM)


def in_vmem(value):
    return pltpu.with_memory_space_constraint(value, pltpu.VMEM)


def after(value, *others):
    return lax.optimization_barrier((value, *others))[0]


def weight_copies(pos, jobs, layers, wd_hbm, w_ref, sems):
    half = w_ref.shape[-1]
    bits = layers.bit_length() - 1
    copies, live = [], []
    for i, (slot, part) in enumerate(jobs):
        side = (pos[0] & 1) if part == 0 else 1 - (pos[0] & 1)
        target = (pos[0] >> 1) ^ slot_offset(slot, side, bits)
        cols = pl.ds(pl.multiple_of(side * half, half), half)
        copies.append(pltpu.make_async_copy(wd_hbm.at[target, :, cols], w_ref.at[i], sems.at[i]))
        live.append(target >= (pos[0] >> 1))
    return copies, live


def partial_sums(copies, live, act, w_ref, out_refs):
    for i, out_ref in enumerate(out_refs):
        copies[i].wait()

        @pl.when(live[i])
        def _():
            out_ref[...] = jnp.dot(act, w_ref[i], preferred_element_type=F32).astype(out_ref.dtype)

        @pl.when(jnp.logical_not(live[i]))
        def _():
            out_ref[...] = jnp.zeros_like(out_ref)


def job_shapes(jobs, toks, half):
    return [pltpu.VMEM((toks, half), F32 if part == 0 else BF16) for _, part in jobs]


def encode(pos, x, w_enc, b_enc, w_dec, jobs):
    layers, width, cols = w_dec.shape
    toks, half = x.shape[0], cols // 2
    pieces = 3 if cols % (3 * 128) == 0 else 1
    rows = cols // pieces

    def kernel(pos, x_hbm, we_hbm, b_hbm, wd_hbm, pre_ref, act_ref, act_t_ref, *refs):
        out_refs, (w_ref, x_ref, we_ref, b_ref, sems, w_sems) = refs[: len(jobs)], refs[len(jobs):]
        loads = [pltpu.make_async_copy(b_hbm, b_ref, sems.at[0])]
        for i in range(pieces):
            span = pl.ds(i * rows, rows)
            loads.append(pltpu.make_async_copy(x_hbm.at[:, span], x_ref.at[:, span], sems.at[2 * i + 1]))
            loads.append(pltpu.make_async_copy(we_hbm.at[span], we_ref.at[span], sems.at[2 * i + 2]))
        for load in loads:
            load.start()
        copies, live = weight_copies(pos, jobs, layers, wd_hbm, w_ref, w_sems)
        for copy in copies:
            copy.start()
        loads[0].wait()
        pre = jnp.broadcast_to(b_ref[...], (toks, width))
        for i in range(pieces):
            loads[2 * i + 1].wait()
            loads[2 * i + 2].wait()
            span = pl.ds(i * rows, rows)
            pre += jnp.dot(x_ref[:, span], we_ref[span], preferred_element_type=F32)
        pre_ref[...] = pre
        act = jnp.maximum(pre, 0.0).astype(BF16)
        act_ref[...] = act
        partial_sums(copies, live, act, w_ref, out_refs)
        act_t_ref[...] = act.T

    out = pl.pallas_call(
        kernel,
        in_specs=[IN_SMEM] + [IN_PLACE] * 4,
        out_specs=[IN_VMEM] * (3 + len(jobs)),
        out_shape=[
            pltpu.VMEM((toks, width), F32),
            pltpu.VMEM((toks, width), BF16),
            pltpu.VMEM((width, toks), BF16),
        ]
        + job_shapes(jobs, toks, half),
        scratch_shapes=[
            pltpu.VMEM((len(jobs), width, half), BF16),
            pltpu.VMEM(x.shape, BF16),
            pltpu.VMEM(w_enc.shape, BF16),
            pltpu.VMEM(b_enc.shape, F32),
            pltpu.SemaphoreType.DMA((2 * pieces + 1,)),
            pltpu.SemaphoreType.DMA((len(jobs),)),
        ],
        **params(),
    )(pos, in_hbm(x), in_hbm(w_enc), in_hbm(b_enc), in_hbm(w_dec))
    return out[0], out[1], out[2], dict(zip(jobs, out[3:]))


def decode(pos, act, w_dec, jobs):
    layers, width, cols = w_dec.shape
    toks, half = act.shape[0], cols // 2

    def kernel(pos, act_ref, wd_hbm, *refs):
        out_refs, (w_ref, w_sems) = refs[: len(jobs)], refs[len(jobs):]
        copies, live = weight_copies(pos, jobs, layers, wd_hbm, w_ref, w_sems)
        for copy in copies:
            copy.start()
        partial_sums(copies, live, act_ref[...], w_ref, out_refs)

    out = pl.pallas_call(
        kernel,
        in_specs=[IN_SMEM, IN_VMEM, IN_PLACE],
        out_specs=[IN_VMEM] * len(jobs),
        out_shape=job_shapes(jobs, toks, half),
        scratch_shapes=[
            pltpu.VMEM((len(jobs), width, half), BF16),
            pltpu.SemaphoreType.DMA((len(jobs),)),
        ],
        **params(),
    )(pos, in_vmem(act), in_hbm(w_dec))
    return dict(zip(jobs, out))


def backward(pos, jobs, errs, act_t, w_dec, carry, weights=None, ahead=(), last=None, cost=1):
    layers, width, cols = w_dec.shape
    toks, half = errs[0].shape
    bits = layers.bit_length() - 1
    scale = toks ** (-0.5)
    count = len(jobs)
    pieces = 9 if cols % (9 * 128) == 0 else 1

    def kernel(pos, *refs):
        refs = list(refs)
        take = lambda n: [refs.pop(0) for _ in range(n)]
        err_refs, (act_t_ref, wd_hbm) = take(count), take(2)
        old_ref = take(2)[0] if carry is not None else None
        w_refs = take(count) if weights is not None else None
        x_ref, pre_ref = take(2) if last is not None else (None, None)
        sum_ref = take(1)[0] if last is None else None
        grad_hbm = take(1)[0]
        ahead_refs = take(len(ahead))
        genc_hbm, gb_hbm = take(2) if last is not None else (None, None)
        grad_ref, grad_sems = take(2)
        load_ref, load_sems = take(2) if weights is None else (None, None)
        ahead_sems = take(1)[0] if ahead else None
        genc_ref, gb_ref, total_ref, enc_sems = take(4) if last is not None else (None,) * 4

        def place(slot, part):
            side = (pos[0] & 1) if part == 0 else 1 - (pos[0] & 1)
            target = (pos[0] >> 1) ^ slot_offset(slot, side, bits)
            return target, pl.ds(pl.multiple_of(side * half, half), half)

        loads, writes, live, later = [], [], [], []
        for i, job in enumerate(jobs):
            target, span = place(*job)
            live.append(target >= (pos[0] >> 1))
            writes.append(pltpu.make_async_copy(grad_ref.at[i], grad_hbm.at[target, :, span], grad_sems.at[i]))
            if weights is None:
                loads.append(pltpu.make_async_copy(wd_hbm.at[target, :, span], load_ref.at[i], load_sems.at[i]))
        for i, job in enumerate(ahead):
            target, span = place(*job)
            later.append(pltpu.make_async_copy(wd_hbm.at[target, :, span], ahead_refs[i], ahead_sems.at[i]))
        for copy in loads + later:
            copy.start()
        if weights is None:
            w_refs = [load_ref.at[i] for i in range(count)]

        if last is not None:
            sum_ref = total_ref
        sum_ref[...] = jnp.zeros_like(sum_ref) if carry is None else old_ref[...]
        for i in range(count):

            @pl.when(live[i])
            def _():
                grad = jnp.dot(act_t_ref[...], err_refs[i][...], preferred_element_type=F32)
                grad_ref[i] = (grad * scale).astype(BF16)

            @pl.when(jnp.logical_not(live[i]))
            def _():
                grad_ref[i] = jnp.zeros((width, half), BF16)

            writes[i].start()
        for i in range(count):
            if weights is None:
                loads[i].wait()

            @pl.when(live[i])
            def _():
                sum_ref[...] += lax.dot_general(
                    err_refs[i][...], w_refs[i][...], (((1,), (1,)), ((), ())), preferred_element_type=F32
                )

        if last is not None:
            pre_grad = jnp.where(pre_ref[...] > 0, sum_ref[...] * scale, 0.0).astype(BF16)
            gb_ref[...] = jnp.sum(pre_grad.astype(F32), axis=0, keepdims=True)
            writes.append(pltpu.make_async_copy(gb_ref, gb_hbm, enc_sems.at[pieces]))
            writes[-1].start()
            for i in range(pieces):
                span = pl.ds(i * (cols // pieces), cols // pieces)
                genc_ref[span] = lax.dot_general(
                    x_ref[:, span], pre_grad, (((0,), (0,)), ((), ())), preferred_element_type=F32
                ).astype(BF16)
                write = pltpu.make_async_copy(genc_ref.at[span], genc_hbm.at[span], enc_sems.at[i])
                write.start()
                writes.append(write)
        for copy in later + writes:
            copy.wait()

    in_specs = [IN_SMEM] + [IN_VMEM] * (count + 1) + [IN_PLACE]
    args = [pos] + [in_vmem(a) for a in (*errs, act_t)] + [in_hbm(w_dec)]
    sums = 0 if last is not None else 1
    out_specs = [IN_VMEM] * sums + [IN_PLACE] + [IN_VMEM] * len(ahead)
    out_shape = [pltpu.VMEM((toks, width), F32)] * sums + [pltpu.HBM((layers, width, cols), BF16)]
    out_shape += [pltpu.VMEM((width, half), BF16)] * len(ahead)
    scratch = [pltpu.VMEM((count, width, half), BF16), pltpu.SemaphoreType.DMA((count,))]
    aliases = {}
    if carry is not None:
        in_specs += [IN_VMEM, IN_PLACE]
        args += [in_vmem(carry[0]), carry[1]]
        aliases = {len(args) - 1: sums}
    if weights is None:
        scratch += [pltpu.VMEM((count, width, half), BF16), pltpu.SemaphoreType.DMA((count,))]
    else:
        in_specs += [IN_VMEM] * count
        args += [in_vmem(a) for a in weights]
    if ahead:
        scratch += [pltpu.SemaphoreType.DMA((len(ahead),))]
    if last is not None:
        in_specs += [IN_VMEM] * 2
        args += [in_vmem(a) for a in last]
        out_specs += [IN_PLACE] * 2
        out_shape += [pltpu.HBM((cols, width), BF16), pltpu.HBM((1, width), F32)]
        scratch += [
            pltpu.VMEM((cols, width), BF16),
            pltpu.VMEM((1, width), F32),
            pltpu.VMEM((toks, width), F32),
            pltpu.SemaphoreType.DMA((pieces + 1,)),
        ]
    return pl.pallas_call(
        kernel,
        in_specs=in_specs,
        out_specs=out_specs,
        out_shape=out_shape,
        scratch_shapes=scratch,
        input_output_aliases=aliases,
        **params(cost),
    )(*args)


def add_up(values, dtype, cost=1):
    def kernel(*refs):
        total = refs[0][...].astype(F32)
        for ref in refs[1:-1]:
            total += ref[...].astype(F32)
        refs[-1][...] = total.astype(dtype)

    return pl.pallas_call(
        kernel,
        in_specs=[IN_VMEM] * len(values),
        out_specs=IN_VMEM,
        out_shape=pltpu.VMEM(values[0].shape, dtype),
        **params(cost),
    )(*[in_vmem(v) for v in values])


def add_rows(high, parts, whole, pieces, dtype):
    n, cols = whole[0].shape[0] // 2, whole[0].shape[1]

    def kernel(high, *refs):
        rest = list(refs[len(whole):])
        for i, part in enumerate(parts):
            start = (high[0] if part == 0 else 1 - high[0]) * n
            total = jnp.zeros((n, cols), F32)
            for ref in refs[: len(whole)]:
                total += ref[pl.ds(pl.multiple_of(start, n), n)].astype(F32)
            for _ in pieces[i]:
                total += rest.pop(0)[...].astype(F32)
            refs[i - len(parts)][...] = total.astype(dtype)

    values = [*whole, *[p for group in pieces for p in group]]
    return pl.pallas_call(
        kernel,
        in_specs=[IN_SMEM] + [IN_VMEM] * len(values),
        out_specs=[IN_VMEM] * len(parts),
        out_shape=[pltpu.VMEM((n, cols), dtype)] * len(parts),
        **params(),
    )(high, *[in_vmem(v) for v in values])


def join_rows(high, kept, far, cost=1):
    n, cols = kept.shape

    def kernel(high, kept_ref, far_ref, out_ref):
        out_ref[pl.ds(pl.multiple_of(high[0] * n, n), n)] = kept_ref[...]
        out_ref[pl.ds(pl.multiple_of((1 - high[0]) * n, n), n)] = far_ref[...]

    return pl.pallas_call(
        kernel,
        in_specs=[IN_SMEM] + [IN_VMEM] * 2,
        out_specs=IN_VMEM,
        out_shape=pltpu.VMEM((2 * n, cols), kept.dtype),
        **params(cost),
    )(high, in_vmem(kept), in_vmem(far))


def shards(inputs, targets, w_enc, b_enc, w_dec):
    layers, cols = w_dec.shape[1], w_dec.shape[3]
    feats = lax.axis_size("feat")
    bits, feat_bits = layers.bit_length() - 1, feats.bit_length() - 1
    half = cols // 2
    own_layer, own_feat = lax.axis_index("layer"), lax.axis_index("feat")
    core = own_feat & 1
    pos = (own_layer * 2 + core).astype(jnp.int32).reshape(1)
    x, tgt, wd = inputs[0], targets[0], w_dec[0]

    def swap_feat(value, bit):
        return lax.ppermute(value, "feat", [(f, f ^ (1 << bit)) for f in range(feats)])

    def swap_layer(value, step, cross=False):
        pairs = [
            (l * feats + f, (l ^ (1 << layer_bit(step, f & 1, bits))) * feats + (f ^ 2 if cross else f))
            for l in range(layers)
            for f in range(feats)
        ]
        return lax.ppermute(value, ("layer", "feat"), pairs)

    def jobs(low, high):
        return [(s, part) for s in reversed(range(low, high)) for part in (1, 0)]

    mid, final = layers // 2, layers - 1
    high = ((own_feat >> 1) & 1).reshape(1)
    pre, act, act_t, sums = encode(pos, x, w_enc[0], b_enc, wd, [(final, 1)])
    got = {final: swap_feat(sums[final, 1], 0)}
    sums |= decode(pos, act, wd, [(final, 0)] + [(s, 1) for s in reversed(range(mid, final))])
    for s in reversed(range(mid, final)):
        got[s] = swap_feat(sums[s, 1], 0)
    away = add_up([sums[final, 0], got[final]], BF16)
    slots = [[] for _ in range(mid)]
    slots[final - mid].append(swap_layer(away, 0))
    sums |= decode(pos, after(act, away), wd, [(s, 0) for s in reversed(range(mid, final))] + jobs(0, mid))
    for s in reversed(range(mid)):
        got[s] = swap_feat(sums[s, 1], 0)
        slots[s] += [sums[s, 0], got[s]]
    for s in range(mid, final):
        slots.append([after(sums[s, 0], sums[0, 0]), got[s]])
    tgt = after(tgt, away)
    rows = []
    for step in range(bits):
        n = layers >> (step + 1)
        for s in reversed(range(n)):
            if step == 0 and n + s == final:
                continue
            if s > 0 or step < bits - 1:
                slots[s].append(swap_layer(add_up(slots[n + s], BF16), step))
            else:
                kept, away = add_rows(high, (0, 1), slots[n], ([], []), BF16)
                rows += [swap_layer(kept, step), add_up([swap_layer(away, step, cross=True)], BF16, 100000000000)]

    pair_tgt = swap_feat(tgt, 0)
    pair = jnp.where(core == 0, jnp.stack([tgt, pair_tgt]), jnp.stack([pair_tgt, tgt]))
    pair = -jnp.concatenate([pair[0], pair[1]], axis=1)
    span = pair.shape[1]
    chip, chips = own_feat >> 1, feats // 2
    spread = jnp.zeros((x.shape[0], half), BF16)
    for i in range(chips // 2):
        padded = jnp.pad(pair, ((0, 0), (i * span, half - (i + 1) * span)))
        spread = jnp.where(chip == core * (chips // 2) + i, padded, spread)

    (away,) = add_rows(high, (1,), [*slots[0], after(spread, kept)], ([],), BF16)
    rows.append(swap_feat(away, 1))
    (rows,) = add_rows(high, (0,), [*slots[0], spread], (rows,), F32)
    for bit in range(2, feat_bits - 1):
        n = rows.shape[0] // 2
        upper = ((own_feat >> bit) & 1) == 1
        away = jnp.where(upper, rows[:n], rows[n:]).astype(BF16)
        rows = jnp.where(upper, rows[n:], rows[:n]) + swap_feat(away, bit).astype(F32)
    rows = rows + swap_feat(rows.astype(BF16), feat_bits - 1).astype(F32)
    err = rows.astype(BF16)
    for bit in reversed(range(2, feat_bits - 1)):
        upper = ((own_feat >> bit) & 1) == 1
        far = swap_feat(err, bit)
        err = jnp.concatenate([jnp.where(upper, far, err), jnp.where(upper, err, far)])

    near = [swap_layer(err, step) for step in reversed(range(bits))]
    cross = swap_layer(err, bits - 1, cross=True)
    far = swap_feat(err, 1)
    slots = [join_rows(high, err, far)]
    start = backward(pos, [(0, 0)], [slots[0]], act_t, wd, None)
    for i, step in enumerate(reversed(range(bits))):
        for s in range(len(slots)):
            if s > 0:
                slots.append(swap_layer(slots[s], step))
            elif i > 0:
                slots.append(join_rows(high, near[i], swap_layer(far, step), 10000000000))
            else:
                slots.append(join_rows(high, near[i], after(cross, start[0]), 1))
    between = range(2, final)
    work = [(0, 1), (1, 0), (1, 1)] + [(s, 0) for s in between]
    errs = [swap_feat(slots[0], 0), slots[1], swap_feat(slots[1], 0)] + [slots[s] for s in between]
    others = [swap_feat(slots[s], 0) for s in between]
    rest = [(s, 1) for s in between] + [(final, 0)]
    carry = backward(pos, work, errs, act_t, wd, start, ahead=rest + [(final, 1)])
    carry, w_rest, w_last = carry[:2], carry[2:-1], carry[-1]
    others.append(swap_feat(after(slots[final], carry[0]), 0))
    carry = backward(pos, rest, [*others[:-1], slots[final]], act_t, wd, carry, w_rest)
    carry = backward(pos, [(final, 1)], others[-1:], act_t, wd, carry, [w_last], last=(x, pre))
    grad_dec, grad_enc, grad_benc = carry
    return grad_enc[None], grad_dec[None], grad_benc


def solution(mesh):
    in_specs = (
        P("layer", None, None),
        P("layer", None, "feat"),
        P("layer", None, "feat"),
        P("layer", "feat"),
        P("layer", None, "feat", None),
    )
    out_specs = (P("layer", None, "feat"), P("layer", None, "feat", None), P("layer", "feat"))
    return jax.shard_map(shards, mesh=mesh, in_specs=in_specs, out_specs=out_specs, check_vma=False)
```
